256 devices in a mesh: seq: 128 (over z, y_hi, x, core), user: 2 (over y_lo).
Axes of the slice: x: 4, y: 4 (y_hi: 2, y_lo: 2; y = y_hi * 2 + y_lo), z: 8, core: 2. Of those that a mesh axis runs over, the one named last changes fastest.
Arguments:
- z_input: bfloat16 [2, 131072, 384], P('user', 'seq'), may hold values from -6 to 6
- gate_input: bfloat16 [2, 131072, 384], P('user', 'seq'), may hold values from -6 to 6
- cotangent: bfloat16 [2, 131072, 384], P('user', 'seq'), may hold values from -6 to 6
- spectrum: bfloat16 [2, 2, 128, 1024, 384], P(None, None, 'seq'), may hold values from -6 to 6
- skip_gain: float32 [384], replicated, may hold values from 0.5 to 1.5
- lengths: int32 [2], P('user'), may hold values from 32768 to 131072, as said below
Outputs:
- z_grad: bfloat16 [2, 131072, 384], P('user', 'seq')
- spectrum_grad: float32 [2, 2, 128, 1024, 384], P(None, None, 'seq', 'user')
The draws below stay inside these ranges and needn't reach their ends.
Inputs may be any that keep to these rules, and one draw needn't show every extreme that they name: `lengths`: some user's history has all 131072 events.
All inputs are finite; a program needn't handle non-finite values.
Results may differ from the reference program's by a relative error of at most 0.0049.
Values may be sent and summed in bfloat16 or wider, within the bound.
A program may use at most 128 MiB of HBM per device.

```python
import jax
import jax.numpy as jnp
from jax import lax

SEQ_DEV = 1024
CH = 384
SEQLEN = 131072
FBLK = 128
USERS = 2
N_SEQ = 128


def draw_lengths(key, part):
    key = jax.random.fold_in(key, 7)
    key_lengths, key_choice = jax.random.split(key)
    spread = jax.random.randint(key_lengths, (USERS,), SEQLEN // 4, SEQLEN + 1)
    chosen = jax.random.randint(key_choice, (), 0, USERS)
    return jnp.where(jnp.arange(USERS) == chosen, SEQLEN, spread).astype(jnp.int32)


def levels(rng, dims, cuts, low, top_value):
    def one(axis_at, blocks):
        steps = jax.random.uniform(jax.random.fold_in(jax.random.fold_in(rng, 6), axis_at), (blocks,), jnp.float32, low / len(cuts), top_value / len(cuts))
        return jnp.repeat(jnp.exp(steps), dims[axis_at] // blocks).reshape((-1,) + (1,) * (len(dims) - axis_at - 1))

    level = one(*cuts[0])
    for cut in cuts[1:]:
        level = level * one(*cut)
    return level


def bell_draw(stream_key, shape, scale, reach, cuts=(), kind=jnp.bfloat16):
    result = scale * jax.random.normal(stream_key, shape, jnp.float32)
    if cuts:
        result = result * levels(stream_key, shape, cuts, -0.22, 0.18)
    return jnp.clip(result, -reach, reach).astype(kind)


def setup_inputs(seed: int = 0) -> dict:
    keys = jax.random.split(jax.random.key(seed), 7)
    z_input = bell_draw(keys[0], (USERS, SEQLEN, CH), 1.0, 6.0, ((0, 2), (1, 128)))
    gate_input = bell_draw(keys[1], (USERS, SEQLEN, CH), 1.0, 6.0, ((0, 2), (1, 128)))
    cotangent = bell_draw(keys[2], (USERS, SEQLEN, CH), 1.0, 6.0, ((0, 2), (1, 128)))
    spectrum = bell_draw(keys[3], (2, 2, FBLK, SEQ_DEV, CH), 1.0, 6.0, ((2, 128),))
    skip_gain = jnp.clip(jax.random.uniform(keys[4], (CH,), jnp.float32, 0.5, 1.5), 0.5, 1.5)
    lengths = draw_lengths(jax.random.fold_in(keys[6], 71), 0)
    return dict(z_input=z_input, gate_input=gate_input, cotangent=cotangent, spectrum=spectrum, skip_gain=skip_gain, lengths=lengths)


def channel_terms(pieces):
    z_piece, g_piece, filter_real, filter_imag = pieces
    seq_total = z_piece.shape[0]
    z_hat = jnp.fft.fft(z_piece, n=2 * seq_total, axis=0)
    g_hat = jnp.fft.fft(g_piece, n=2 * seq_total, axis=0)
    product = jnp.conj(filter_real + 1j * filter_imag) * g_hat
    conv = jnp.real(jnp.fft.ifft(product, axis=0))[:seq_total]
    cross = jnp.conj(z_hat) * g_hat / (2 * seq_total)
    return conv, jnp.real(cross), jnp.imag(cross)


def reference(z_input, gate_input, cotangent, spectrum, skip_gain, lengths):
    seq_total = SEQ_DEV * N_SEQ
    channel_count = z_input.shape[2]
    channel_group = 128 if channel_count % 128 == 0 else channel_count
    group_count = channel_count // channel_group
    filter_real = spectrum[:, 0].astype(jnp.float32).transpose(2, 1, 0, 3).reshape(2 * seq_total, channel_count)
    filter_imag = spectrum[:, 1].astype(jnp.float32).transpose(2, 1, 0, 3).reshape(2 * seq_total, channel_count)

    def grouped(array):
        return array.reshape(array.shape[0], group_count, channel_group).transpose(1, 0, 2)

    def ungrouped(array):
        return array.transpose(1, 0, 2).reshape(array.shape[1], channel_count)

    grad_list = []
    grad_real = jnp.zeros((2 * seq_total, channel_count), jnp.float32)
    grad_imag = jnp.zeros((2 * seq_total, channel_count), jnp.float32)
    for user_index in range(USERS):
        alive_rows = (jnp.arange(seq_total, dtype=jnp.int32) < lengths[user_index])[:, None]
        g_rows = jnp.where(alive_rows, cotangent[user_index].astype(jnp.float32) * gate_input[user_index].astype(jnp.float32), 0.0).astype(jnp.bfloat16)
        z_rows = jnp.where(alive_rows, z_input[user_index], jnp.zeros_like(z_input[user_index]))
        conv, cross_real, cross_imag = lax.map(channel_terms, (grouped(z_rows.astype(jnp.float32)), grouped(g_rows.astype(jnp.float32)), grouped(filter_real), grouped(filter_imag)))
        conv = ungrouped(conv)
        grad_real = grad_real + ungrouped(cross_real)
        grad_imag = grad_imag + ungrouped(cross_imag)
        grad_rows = jnp.where(alive_rows, skip_gain[None, :] * g_rows.astype(jnp.float32) + conv, 0.0).astype(jnp.bfloat16)
        grad_list.append(grad_rows)

    def layout(array):
        return array.reshape(SEQ_DEV, N_SEQ, 2, channel_count).transpose(2, 1, 0, 3)

    spectrum_grad = jnp.stack([layout(grad_real), layout(grad_imag)], axis=1).astype(jnp.float32)
    return jnp.stack(grad_list), spectrum_grad
```

```python
import functools

import jax
import jax.numpy as jnp
import ml_dtypes
import numpy as np
from jax import lax
from jax.experimental import pallas as pl
from jax.experimental.pallas import tpu as pltpu
from jax.sharding import PartitionSpec as P

LANES = 128
SUB = 8
PER = 3


def split_bf16(values):
    high = values.astype(ml_dtypes.bfloat16)
    low = (values - high.astype(np.float64)).astype(ml_dtypes.bfloat16)
    return high, low


def tables(n_seq):
    rows = SUB * n_seq
    total = rows * LANES
    index = np.arange(rows)
    freq = (index // SUB) + n_seq * (index % SUB)
    outer, turn = [], []
    for parity in range(2):
        twice = 2 * freq + parity
        angle = (twice[:, None] * index[None, :]) % (2 * rows) * (np.pi / rows)
        outer.append(np.concatenate([np.cos(angle), -np.sin(angle)], 0))
        small = twice[:, None] * np.arange(LANES)[None, :] * (np.pi / total)
        turn.append(np.stack([np.cos(small), -np.sin(small)]))
    outer = np.stack(outer)
    high, low = split_bf16(outer)
    back = np.ascontiguousarray(high.transpose(0, 2, 1))
    lane = np.arange(LANES)
    angle = (lane[:, None] * lane[None, :]) % LANES * (2 * np.pi / LANES)
    cos, sin = np.cos(angle), np.sin(angle)
    forward = np.block([[cos, -sin], [sin, cos]])
    inverse = np.block([[cos, sin], [-sin, cos]])
    fwd_high, fwd_low = split_bf16(forward)
    inv_high, inv_low = split_bf16(inverse)
    inner = np.stack([fwd_high, fwd_low, inv_high, inv_low])
    return high, low, back, np.stack(turn).astype(np.float32), inner


def order(step, n_seq):
    if n_seq % 8:
        return step
    return lax.rem(lax.rem(step, 8) * 3, 8) * (n_seq // 8) + step // 8


def kernel(
    n_seq,
    zg_ref,
    h_ref,
    high_ref,
    low_ref,
    back_ref,
    turn_ref,
    inner_ref,
    s_out,
    c_out,
    zbuf,
    hbuf,
    m_high,
    m_low,
    m_back,
    m_turn,
    m_inner,
    x_buf,
    g_buf,
    b_buf,
    s_send,
    c_part,
    c_other,
    c_send,
    table_sems,
    send_sems,
    recv_sems,
):
    rows = SUB * n_seq
    block = min(256, rows)
    groups = block // SUB
    blocks = rows // block
    scale = 1.0 / (2.0 * rows * LANES)
    seq = lax.axis_index("seq")
    user = lax.axis_index("user")
    core = lax.rem(seq, 2)
    place = seq // 2
    chip = place * 2 + user

    def at_chip(target, which):
        return {"seq": (target // 2) * 2 + which, "user": lax.rem(target, 2)}

    def remote(src, dst, which, device):
        return pltpu.make_async_remote_copy(
            src_ref=src,
            dst_ref=dst,
            send_sem=send_sems.at[which],
            recv_sem=recv_sems.at[which],
            device_id=device,
            device_id_type=pl.DeviceIdType.MESH,
        )

    def scatter(which, src, dst):
        def put(target):
            remote(src.at[target], dst.at[seq], which, at_chip(target, user)).start()

        @pl.when(core == user)
        def _():
            pltpu.make_async_copy(src.at[chip], dst.at[seq], recv_sems.at[which]).start()

        @pl.when(core != user)
        def _():
            put(chip)

        def body(step, carry):
            put(lax.rem(chip + order(step, n_seq), n_seq))
            return carry

        lax.fori_loop(1, n_seq, body, 0)

    def await_all(ref, sem):
        pltpu.make_async_copy(ref, ref, sem).wait()

    def await_sent(which, src):
        @pl.when(core == user)
        def _():
            await_all(src.at[pl.ds(0, n_seq - 1)], send_sems.at[which])

        @pl.when(core != user)
        def _():
            await_all(src, send_sems.at[which])

    scatter(0, zg_ref, zbuf.at[user])
    scatter(1, h_ref, hbuf)

    loads = [
        pltpu.make_async_copy(high_ref.at[core], m_high, table_sems.at[0]),
        pltpu.make_async_copy(low_ref.at[core], m_low, table_sems.at[1]),
        pltpu.make_async_copy(back_ref.at[core], m_back, table_sems.at[2]),
        pltpu.make_async_copy(turn_ref.at[core], m_turn, table_sems.at[3]),
        pltpu.make_async_copy(inner_ref, m_inner, table_sems.at[4]),
    ]
    for load in loads:
        load.start()
    for load in loads:
        load.wait()

    mate = {"seq": seq + 1 - 2 * core, "user": user}
    await_all(zbuf.at[core], recv_sems.at[0])
    swap = remote(zbuf.at[core], zbuf.at[core], 2, mate)
    swap.start()
    swap.wait()

    def forward(channel, carry):
        def fill(part, inner_carry):
            for who in range(2):
                tile = zbuf[who, pl.ds(part * groups, groups), channel]
                tile = tile.astype(jnp.float32)
                at = pl.ds(pl.multiple_of(part * block, block), block)
                for kind in range(2):
                    piece = tile[:, kind * SUB : (kind + 1) * SUB, :]
                    piece = piece.reshape(block, LANES).astype(jnp.bfloat16)
                    left = (2 * who + kind) * LANES
                    x_buf[at, left : left + LANES] = piece
            return inner_carry

        lax.fori_loop(0, blocks, fill, 0)

        def spectrum(part, inner_carry):
            start = pl.multiple_of(part * block, block)
            at = pl.ds(start, block)
            below = pl.ds(pl.multiple_of(rows + part * block, block), block)
            x = x_buf[...]
            dot = functools.partial(jnp.dot, preferred_element_type=jnp.float32)
            y_real = dot(m_high[at, :], x) + dot(m_low[at, :], x)
            y_imag = dot(m_high[below, :], x) + dot(m_low[below, :], x)
            t_real, t_imag = m_turn[0, at, :], m_turn[1, at, :]
            s_real = s_imag = None
            for who in range(2):
                spectra = []
                for kind in range(2):
                    left = (2 * who + kind) * LANES
                    a_real = y_real[:, left : left + LANES]
                    a_imag = y_imag[:, left : left + LANES]
                    mid = jnp.concatenate(
                        [a_real * t_real - a_imag * t_imag, a_real * t_imag + a_imag * t_real],
                        axis=1,
                    ).astype(jnp.bfloat16)
                    spectra.append(dot(mid, m_inner[0]) + dot(mid, m_inner[1]))
                z, g = spectra
                g_buf[channel, who, at, :] = g
                z_real, z_imag = z[:, :LANES], z[:, LANES:]
                g_real, g_imag = g[:, :LANES], g[:, LANES:]
                c_real = z_real * g_real + z_imag * g_imag
                c_imag = z_real * g_imag - z_imag * g_real
                s_real = c_real if who == 0 else s_real + c_real
                s_imag = c_imag if who == 0 else s_imag + c_imag
            s_real, s_imag = s_real * scale, s_imag * scale
            half = LANES // 2
            for who in range(2):
                cut = slice(who * half, (who + 1) * half)
                out = jnp.concatenate([s_real[:, cut], s_imag[:, cut]], axis=1)
                out = out.reshape(groups, SUB, LANES).astype(jnp.bfloat16)
                s_send[pl.ds(who * n_seq + part * groups, groups), channel] = out
            return inner_carry

        lax.fori_loop(0, blocks, spectrum, 0)
        return carry

    lax.fori_loop(0, PER, forward, 0)

    slot = 2 * chip + core

    def put_s(step):
        target = lax.rem(chip + order(step // 2, n_seq), n_seq)
        which = lax.rem(step, 2)
        owner = (target // 2) * 2 + which
        there = lax.rem(target, 2)
        src = s_send.at[there * n_seq + owner]
        remote(src, s_out.at[slot], 3, {"seq": owner, "user": there}).start()

    pltpu.make_async_copy(s_send.at[user * n_seq + seq], s_out.at[slot], recv_sems.at[3]).start()
    put_s(1 - core)

    def body_s(step, carry):
        put_s(step)
        return carry

    lax.fori_loop(2, 2 * n_seq, body_s, 0)

    await_all(hbuf, recv_sems.at[1])

    def inverse(channel, carry):
        dot = functools.partial(jnp.dot, preferred_element_type=jnp.float32)

        def product(part, inner_carry):
            at = pl.ds(pl.multiple_of(part * block, block), block)
            below = pl.ds(pl.multiple_of(rows + part * block, block), block)
            tile = hbuf[pl.ds(part * groups, groups), channel].astype(jnp.float32)
            h_real = tile[:, :SUB, :].reshape(block, LANES)
            h_imag = tile[:, SUB:, :].reshape(block, LANES)
            t_real, t_imag = m_turn[0, at, :], m_turn[1, at, :]
            for who in range(2):
                g = g_buf[channel, who, at, :]
                g_real, g_imag = g[:, :LANES], g[:, LANES:]
                q = jnp.concatenate(
                    [h_real * g_real + h_imag * g_imag, h_real * g_imag - h_imag * g_real],
                    axis=1,
                ).astype(jnp.bfloat16)
                b = dot(q, m_inner[2]) + dot(q, m_inner[3])
                b_real, b_imag = b[:, :LANES], b[:, LANES:]
                left = who * LANES
                b_buf[at, left : left + LANES] = (b_real * t_real + b_imag * t_imag).astype(
                    jnp.bfloat16
                )
                b_buf[below, left : left + LANES] = (b_imag * t_real - b_real * t_imag).astype(
                    jnp.bfloat16
                )
            return inner_carry

        lax.fori_loop(0, blocks, product, 0)

        def fold(part, inner_carry):
            at = pl.ds(pl.multiple_of(part * block, block), block)
            conv = dot(m_back[at, :], b_buf[...]) * scale
            for who in range(2):
                piece = conv[:, who * LANES : (who + 1) * LANES]
                c_part[who, pl.ds(part * groups, groups), channel] = piece.reshape(
                    groups, SUB, LANES
                )
            return inner_carry

        lax.fori_loop(0, blocks, fold, 0)
        return carry

    lax.fori_loop(0, PER, inverse, 0)

    swap_back = remote(c_part.at[1 - core], c_other, 4, mate)
    swap_back.start()
    swap_back.wait()

    def join(part, carry):
        at = pl.ds(part * groups, groups)
        c_send[at] = (c_part[core, at] + c_other[at]).astype(jnp.bfloat16)
        return carry

    lax.fori_loop(0, blocks, join, 0)

    def put_c(target):
        remote(c_send.at[target], c_out.at[chip], 5, {"seq": target, "user": core}).start()

    @pl.when(core == user)
    def _():
        pltpu.make_async_copy(c_send.at[seq], c_out.at[chip], recv_sems.at[5]).start()

    @pl.when(core != user)
    def _():
        put_c(seq)

    def body_c(step, carry):
        put_c(lax.rem(seq + order(step, n_seq), n_seq))
        return carry

    lax.fori_loop(1, n_seq, body_c, 0)

    await_sent(0, zg_ref)
    await_sent(1, h_ref)
    await_all(s_send.at[pl.ds(0, 2 * n_seq - 1)], send_sems.at[3])
    await_sent(5, c_send)
    await_all(s_out, recv_sems.at[3])
    await_all(c_out, recv_sems.at[5])


def mixer(n_seq, zg, h):
    rows = SUB * n_seq
    bf16 = jnp.bfloat16
    high, low, back, turn, inner = (jnp.asarray(t) for t in tables(n_seq))
    anywhere = pl.BlockSpec(memory_space=pl.ANY)
    return pl.pallas_call(
        functools.partial(kernel, n_seq),
        out_shape=(
            jax.ShapeDtypeStruct((2 * n_seq, PER, SUB, LANES), bf16),
            jax.ShapeDtypeStruct((n_seq, PER, SUB, LANES), bf16),
        ),
        in_specs=[anywhere] * 7,
        out_specs=(anywhere, anywhere),
        scratch_shapes=[
            pltpu.VMEM((2, n_seq, PER, 2 * SUB, LANES), bf16),
            pltpu.VMEM((n_seq, PER, 2 * SUB, LANES), bf16),
            pltpu.VMEM((2 * rows, rows), bf16),
            pltpu.VMEM((2 * rows, rows), bf16),
            pltpu.VMEM((rows, 2 * rows), bf16),
            pltpu.VMEM((2, rows, LANES), jnp.float32),
            pltpu.VMEM((4, 2 * LANES, 2 * LANES), bf16),
            pltpu.VMEM((rows, 4 * LANES), bf16),
            pltpu.VMEM((PER, 2, rows, 2 * LANES), jnp.float32),
            pltpu.VMEM((2 * rows, 2 * LANES), bf16),
            pltpu.VMEM((2 * n_seq, PER, SUB, LANES), bf16),
            pltpu.VMEM((2, n_seq, PER, SUB, LANES), jnp.float32),
            pltpu.VMEM((n_seq, PER, SUB, LANES), jnp.float32),
            pltpu.VMEM((n_seq, PER, SUB, LANES), bf16),
            pltpu.SemaphoreType.DMA((5,)),
            pltpu.SemaphoreType.DMA((6,)),
            pltpu.SemaphoreType.DMA((6,)),
        ],
        compiler_params=pltpu.CompilerParams(
            has_side_effects=True, vmem_limit_bytes=58 * 1024 * 1024
        ),
    )(zg, h, high, low, back, turn, inner)


def on_device(z_input, gate_input, cotangent, spectrum, skip_gain, lengths):
    n_seq = lax.axis_size("seq")
    my_seq = lax.axis_index("seq")
    my_user = lax.axis_index("user")
    span, channels = z_input.shape[1:]
    times = my_seq * span + jnp.arange(span, dtype=jnp.int32)
    alive = (times < lengths[0])[:, None]
    grad = jnp.where(
        alive, cotangent[0].astype(jnp.float32) * gate_input[0].astype(jnp.float32), 0.0
    ).astype(jnp.bfloat16)
    masked = jnp.where(alive, z_input[0], jnp.zeros_like(z_input[0]))
    zg = jnp.stack([masked, grad]).reshape(2 * SUB, LANES, channels)
    zg = zg.transpose(2, 0, 1).reshape(n_seq, PER, 2 * SUB, LANES)
    h = lax.dynamic_index_in_dim(spectrum[:, :, 0], my_user, 0, keepdims=False)
    h = h.reshape(2, LANES, SUB, channels).transpose(3, 0, 2, 1)
    h = h.reshape(n_seq, PER, 2 * SUB, LANES)
    s_rows, conv_rows = mixer(n_seq, zg, h)
    s_rows = s_rows.reshape(n_seq, 2, PER, SUB, 2, LANES // 2)
    s_rows = s_rows.transpose(1, 4, 5, 3, 0, 2).astype(jnp.float32)
    spectrum_grad = s_rows.reshape(2, 2, 1, span // 2, channels)
    conv = conv_rows.reshape(channels, span).transpose(1, 0).astype(jnp.float32)
    z_grad = jnp.where(alive, skip_gain * grad.astype(jnp.float32) + conv, 0.0)
    return (z_grad.astype(jnp.bfloat16)[None], spectrum_grad)


def solution(mesh):
    return jax.shard_map(
        on_device,
        mesh=mesh,
        in_specs=(
            P("user", "seq", None),
            P("user", "seq", None),
            P("user", "seq", None),
            P(None, None, "seq", None, None),
            P(),
            P("user"),
        ),
        out_specs=(P("user", "seq", None), P(None, None, "seq", "user", None)),
        check_vma=False,
    )
```

```python
import functools

import jax
import jax.numpy as jnp
import ml_dtypes
import numpy as np
from jax import lax
from jax.experimental import pallas as pl
from jax.experimental.pallas import tpu as pltpu
from jax.sharding import PartitionSpec as P

LANES = 128
SUB = 8
PER = 3


def split_bf16(values):
    high = values.astype(ml_dtypes.bfloat16)
    low = (values - high.astype(np.float64)).astype(ml_dtypes.bfloat16)
    return high, low


def tables(n_seq):
    rows = SUB * n_seq
    total = rows * LANES
    index = np.arange(rows)
    freq = (index // SUB) + n_seq * (index % SUB)
    outer, turn = [], []
    for parity in range(2):
        twice = 2 * freq + parity
        angle = (twice[:, None] * index[None, :]) % (2 * rows) * (np.pi / rows)
        outer.append(np.concatenate([np.cos(angle), -np.sin(angle)], 0))
        small = twice[:, None] * np.arange(LANES)[None, :] * (np.pi / total)
        turn.append(np.stack([np.cos(small), -np.sin(small)]))
    outer = np.stack(outer)
    high, low = split_bf16(outer)
    back = np.ascontiguousarray(high.transpose(0, 2, 1))
    lane = np.arange(LANES)
    angle = (lane[:, None] * lane[None, :]) % LANES * (2 * np.pi / LANES)
    cos, sin = np.cos(angle), np.sin(angle)
    forward = np.block([[cos, -sin], [sin, cos]])
    inverse = np.block([[cos, sin], [-sin, cos]])
    fwd_high, fwd_low = split_bf16(forward)
    inv_high, inv_low = split_bf16(inverse)
    inner = np.stack([fwd_high, fwd_low, inv_high, inv_low])
    return high, low, back, np.stack(turn).astype(np.float32), inner


def order(step, n_seq):
    if n_seq % 8:
        return step
    return lax.rem(lax.rem(step, 8) * 3, 8) * (n_seq // 8) + step // 8


def kernel(
    n_seq,
    z_hbm,
    gate_hbm,
    cot_hbm,
    h_hbm,
    limit_ref,
    high_ref,
    low_ref,
    back_ref,
    turn_ref,
    inner_ref,
    s_final,
    c_final,
    z_in,
    gate_in,
    cot_in,
    h_in,
    stage,
    wide,
    zg_ref,
    h_ref,
    s_out,
    c_out,
    s_turned,
    c_turned,
    zbuf,
    hbuf,
    m_high,
    m_low,
    m_back,
    m_turn,
    m_inner,
    x_buf,
    g_buf,
    b_buf,
    s_send,
    c_part,
    c_other,
    c_send,
    input_sems,
    table_sems,
    send_sems,
    recv_sems,
):
    rows = SUB * n_seq
    block = min(256, rows)
    groups = block // SUB
    blocks = rows // block
    scale = 1.0 / (2.0 * rows * LANES)
    seq = lax.axis_index("seq")
    user = lax.axis_index("user")
    core = lax.rem(seq, 2)
    place = seq // 2
    chip = place * 2 + user

    def at_chip(target, which):
        return {"seq": (target // 2) * 2 + which, "user": lax.rem(target, 2)}

    def remote(src, dst, which, device):
        return pltpu.make_async_remote_copy(
            src_ref=src,
            dst_ref=dst,
            send_sem=send_sems.at[which],
            recv_sem=recv_sems.at[which],
            device_id=device,
            device_id_type=pl.DeviceIdType.MESH,
        )

    def scatter(which, src, dst):
        def put(target):
            remote(src.at[target], dst.at[seq], which, at_chip(target, user)).start()

        @pl.when(core == user)
        def _():
            pltpu.make_async_copy(src.at[chip], dst.at[seq], recv_sems.at[which]).start()

        @pl.when(core != user)
        def _():
            put(chip)

        def body(step, carry):
            put(lax.rem(chip + order(step, n_seq), n_seq))
            return carry

        lax.fori_loop(1, n_seq, body, 0)

    def await_all(ref, sem):
        pltpu.make_async_copy(ref, ref, sem).wait()

    def await_sent(which, src):
        @pl.when(core == user)
        def _():
            await_all(src.at[pl.ds(0, n_seq - 1)], send_sems.at[which])

        @pl.when(core != user)
        def _():
            await_all(src, send_sems.at[which])

    inputs = [
        pltpu.make_async_copy(z_hbm.at[0], z_in, input_sems.at[0]),
        pltpu.make_async_copy(gate_hbm.at[0], gate_in, input_sems.at[1]),
        pltpu.make_async_copy(cot_hbm.at[0], cot_in, input_sems.at[2]),
        pltpu.make_async_copy(h_hbm.at[user, :, 0], h_in, input_sems.at[3]),
    ]
    loads = [
        pltpu.make_async_copy(high_ref.at[core], m_high, table_sems.at[0]),
        pltpu.make_async_copy(low_ref.at[core], m_low, table_sems.at[1]),
        pltpu.make_async_copy(back_ref.at[core], m_back, table_sems.at[2]),
        pltpu.make_async_copy(turn_ref.at[core], m_turn, table_sems.at[3]),
        pltpu.make_async_copy(inner_ref, m_inner, table_sems.at[4]),
    ]
    for load in inputs + loads:
        load.start()

    channels = PER * n_seq
    width = min(LANES, channels)
    columns = channels // width

    def pack(dst):
        def body(part, carry):
            tile = stage[pl.ds(pl.multiple_of(part * 16 * SUB * PER * 2, 8), 16 * SUB * PER * 2), :]
            dst[pl.ds(part * 16, 16)] = tile.reshape(16, PER, 2 * SUB, LANES).astype(jnp.bfloat16)
            return carry

        lax.fori_loop(0, n_seq // 16, body, 0)

    for load in inputs[:3]:
        load.wait()

    def turn_zg(part, carry):
        at = pl.ds(pl.multiple_of(part * LANES, LANES), LANES)
        times = seq * (SUB * LANES) + part * LANES
        times = times + lax.broadcasted_iota(jnp.int32, (LANES, channels), 0)
        alive = times < limit_ref[0]
        z = jnp.where(alive, z_in[at, :].astype(jnp.float32), 0.0)
        g = cot_in[at, :].astype(jnp.float32) * gate_in[at, :].astype(jnp.float32)
        g = jnp.where(alive, g, 0.0)
        for column in range(columns):
            cut = slice(column * width, (column + 1) * width)
            first = column * width * 2 * SUB + part
            stage[pl.ds(first, width, stride=2 * SUB), :] = z[:, cut].T
            stage[pl.ds(first + SUB, width, stride=2 * SUB), :] = g[:, cut].T
        return carry

    lax.fori_loop(0, SUB, turn_zg, 0)
    pack(zg_ref)
    scatter(0, zg_ref, zbuf.at[user])

    inputs[3].wait()
    for kind in range(2):
        for column in range(columns):
            cut = slice(column * width, (column + 1) * width)
            wide[column, :, :width] = h_in[kind, :, cut].astype(jnp.float32)

        def turn_h(low_bits, carry, kind=kind):
            for column in range(columns):
                tile = wide[column, pl.ds(low_bits, LANES, stride=SUB), :]
                first = column * width * 2 * SUB + kind * SUB + low_bits
                stage[pl.ds(first, width, stride=2 * SUB), :] = tile.T[:width]
            return carry

        lax.fori_loop(0, SUB, turn_h, 0)
    pack(h_ref)
    scatter(1, h_ref, hbuf)

    for load in loads:
        load.wait()

    mate = {"seq": seq + 1 - 2 * core, "user": user}
    await_all(zbuf.at[core], recv_sems.at[0])
    swap = remote(zbuf.at[core], zbuf.at[core], 2, mate)
    swap.start()
    swap.wait()

    def forward(channel, carry):
        def fill(part, inner_carry):
            for who in range(2):
                tile = zbuf[who, pl.ds(part * groups, groups), channel]
                tile = tile.astype(jnp.float32)
                at = pl.ds(pl.multiple_of(part * block, block), block)
                for kind in range(2):
                    piece = tile[:, kind * SUB : (kind + 1) * SUB, :]
                    piece = piece.reshape(block, LANES).astype(jnp.bfloat16)
                    left = (2 * who + kind) * LANES
                    x_buf[at, left : left + LANES] = piece
            return inner_carry

        lax.fori_loop(0, blocks, fill, 0)

        def spectrum(part, inner_carry):
            start = pl.multiple_of(part * block, block)
            at = pl.ds(start, block)
            below = pl.ds(pl.multiple_of(rows + part * block, block), block)
            x = x_buf[...]
            dot = functools.partial(jnp.dot, preferred_element_type=jnp.float32)
            y_real = dot(m_high[at, :], x) + dot(m_low[at, :], x)
            y_imag = dot(m_high[below, :], x) + dot(m_low[below, :], x)
            t_real, t_imag = m_turn[0, at, :], m_turn[1, at, :]
            s_real = s_imag = None
            for who in range(2):
                spectra = []
                for kind in range(2):
                    left = (2 * who + kind) * LANES
                    a_real = y_real[:, left : left + LANES]
                    a_imag = y_imag[:, left : left + LANES]
                    mid = jnp.concatenate(
                        [a_real * t_real - a_imag * t_imag, a_real * t_imag + a_imag * t_real],
                        axis=1,
                    ).astype(jnp.bfloat16)
                    spectra.append(dot(mid, m_inner[0]) + dot(mid, m_inner[1]))
                z, g = spectra
                g_buf[channel, who, at, :] = g
                z_real, z_imag = z[:, :LANES], z[:, LANES:]
                g_real, g_imag = g[:, :LANES], g[:, LANES:]
                c_real = z_real * g_real + z_imag * g_imag
                c_imag = z_real * g_imag - z_imag * g_real
                s_real = c_real if who == 0 else s_real + c_real
                s_imag = c_imag if who == 0 else s_imag + c_imag
            s_real, s_imag = s_real * scale, s_imag * scale
            half = LANES // 2
            for who in range(2):
                cut = slice(who * half, (who + 1) * half)
                out = jnp.concatenate([s_real[:, cut], s_imag[:, cut]], axis=1)
                out = out.reshape(groups, SUB, LANES).astype(jnp.bfloat16)
                s_send[pl.ds(who * n_seq + part * groups, groups), channel] = out
            return inner_carry

        lax.fori_loop(0, blocks, spectrum, 0)
        return carry

    lax.fori_loop(0, PER, forward, 0)

    slot = core * n_seq + chip

    def put_s(step):
        target = lax.rem(chip + order(step // 2, n_seq), n_seq)
        which = lax.rem(step, 2)
        owner = (target // 2) * 2 + which
        there = lax.rem(target, 2)
        src = s_send.at[there * n_seq + owner]
        remote(src, s_out.at[slot], 3, {"seq": owner, "user": there}).start()

    pltpu.make_async_copy(s_send.at[user * n_seq + seq], s_out.at[slot], recv_sems.at[3]).start()
    put_s(1 - core)

    def body_s(step, carry):
        put_s(step)
        return carry

    lax.fori_loop(2, 2 * n_seq, body_s, 0)

    await_all(hbuf, recv_sems.at[1])

    def inverse(channel, carry):
        dot = functools.partial(jnp.dot, preferred_element_type=jnp.float32)

        def product(part, inner_carry):
            at = pl.ds(pl.multiple_of(part * block, block), block)
            below = pl.ds(pl.multiple_of(rows + part * block, block), block)
            tile = hbuf[pl.ds(part * groups, groups), channel].astype(jnp.float32)
            h_real = tile[:, :SUB, :].reshape(block, LANES)
            h_imag = tile[:, SUB:, :].reshape(block, LANES)
            t_real, t_imag = m_turn[0, at, :], m_turn[1, at, :]
            for who in range(2):
                g = g_buf[channel, who, at, :]
                g_real, g_imag = g[:, :LANES], g[:, LANES:]
                q = jnp.concatenate(
                    [h_real * g_real + h_imag * g_imag, h_real * g_imag - h_imag * g_real],
                    axis=1,
                ).astype(jnp.bfloat16)
                b = dot(q, m_inner[2]) + dot(q, m_inner[3])
                b_real, b_imag = b[:, :LANES], b[:, LANES:]
                left = who * LANES
                b_buf[at, left : left + LANES] = (b_real * t_real + b_imag * t_imag).astype(
                    jnp.bfloat16
                )
                b_buf[below, left : left + LANES] = (b_imag * t_real - b_real * t_imag).astype(
                    jnp.bfloat16
                )
            return inner_carry

        lax.fori_loop(0, blocks, product, 0)

        def fold(part, inner_carry):
            at = pl.ds(pl.multiple_of(part * block, block), block)
            conv = dot(m_back[at, :], b_buf[...]) * scale
            for who in range(2):
                piece = conv[:, who * LANES : (who + 1) * LANES]
                c_part[who, pl.ds(part * groups, groups), channel] = piece.reshape(
                    groups, SUB, LANES
                )
            return inner_carry

        lax.fori_loop(0, blocks, fold, 0)
        return carry

    lax.fori_loop(0, PER, inverse, 0)

    swap_back = remote(c_part.at[1 - core], c_other, 4, mate)
    swap_back.start()
    swap_back.wait()

    def join(part, carry):
        at = pl.ds(part * groups, groups)
        c_send[at] = (c_part[core, at] + c_other[at]).astype(jnp.bfloat16)
        return carry

    lax.fori_loop(0, blocks, join, 0)

    def put_c(target):
        remote(c_send.at[target], c_out.at[chip], 5, {"seq": target, "user": core}).start()

    @pl.when(core == user)
    def _():
        pltpu.make_async_copy(c_send.at[seq], c_out.at[chip], recv_sems.at[5]).start()

    @pl.when(core != user)
    def _():
        put_c(seq)

    def body_c(step, carry):
        put_c(lax.rem(seq + order(step, n_seq), n_seq))
        return carry

    lax.fori_loop(1, n_seq, body_c, 0)

    def unpack(src):
        def body(part, carry):
            tile = src[pl.ds(part * 16, 16)].astype(jnp.float32)
            size = 16 * PER * SUB
            stage[pl.ds(pl.multiple_of(part * size, 8), size), :] = tile.reshape(size, LANES)
            return carry

        lax.fori_loop(0, n_seq // 16, body, 0)

    half = LANES // 2
    await_all(s_out, recv_sems.at[3])
    for parity in range(2):
        unpack(s_out.at[pl.ds(parity * n_seq, n_seq)])

        def turn_s(low_bits, carry):
            for column in range(columns):
                first = column * width * SUB + low_bits
                tile = stage[pl.ds(first, width, stride=SUB), :].T
                for kind in range(2):
                    first = kind * half * SUB + low_bits
                    piece = tile[kind * half : (kind + 1) * half]
                    wide[column, pl.ds(first, half, stride=SUB), :width] = piece
            return carry

        lax.fori_loop(0, SUB, turn_s, 0)
        for column in range(columns):
            cut = slice(column * width, (column + 1) * width)
            for kind in range(2):
                at = pl.ds(kind * half * SUB, half * SUB)
                s_turned[parity, kind, :, cut] = wide[column, at, :width].astype(jnp.bfloat16)
    s_store = pltpu.make_async_copy(s_turned, s_final, input_sems.at[0])
    s_store.start()

    await_all(c_out, recv_sems.at[5])
    unpack(c_out)

    def turn_c(part, carry):
        at = pl.ds(pl.multiple_of(part * LANES, LANES), LANES)
        for column in range(columns):
            first = column * width * SUB + part
            tile = stage[pl.ds(first, width, stride=SUB), :].T
            c_turned[at, column * width : (column + 1) * width] = tile.astype(jnp.bfloat16)
        return carry

    lax.fori_loop(0, SUB, turn_c, 0)
    c_store = pltpu.make_async_copy(c_turned, c_final, input_sems.at[1])
    c_store.start()

    await_sent(0, zg_ref)
    await_sent(1, h_ref)
    await_all(s_send.at[pl.ds(0, 2 * n_seq - 1)], send_sems.at[3])
    await_sent(5, c_send)
    s_store.wait()
    c_store.wait()


def mixer(n_seq, z_input, gate_input, cotangent, spectrum, lengths):
    rows = SUB * n_seq
    span, channels = z_input.shape[1:]
    bf16, f32 = jnp.bfloat16, jnp.float32
    high, low, back, turn, inner = (jnp.asarray(t) for t in tables(n_seq))
    anywhere = pl.BlockSpec(memory_space=pl.ANY)
    return pl.pallas_call(
        functools.partial(kernel, n_seq),
        out_shape=(
            jax.ShapeDtypeStruct((2, 2, span // 2, channels), bf16),
            jax.ShapeDtypeStruct((span, channels), bf16),
        ),
        in_specs=[anywhere] * 4 + [pl.BlockSpec(memory_space=pltpu.SMEM)] + [anywhere] * 5,
        out_specs=(anywhere, anywhere),
        scratch_shapes=[
            pltpu.VMEM((span, channels), bf16),
            pltpu.VMEM((span, channels), bf16),
            pltpu.VMEM((span, channels), bf16),
            pltpu.VMEM((2, span, channels), bf16),
            pltpu.VMEM((channels * 2 * SUB, LANES), f32),
            pltpu.VMEM((max(1, channels // LANES), span, LANES), f32),
            pltpu.VMEM((n_seq, PER, 2 * SUB, LANES), bf16),
            pltpu.VMEM((n_seq, PER, 2 * SUB, LANES), bf16),
            pltpu.VMEM((2 * n_seq, PER, SUB, LANES), bf16),
            pltpu.VMEM((n_seq, PER, SUB, LANES), bf16),
            pltpu.VMEM((2, 2, span // 2, channels), bf16),
            pltpu.VMEM((span, channels), bf16),
            pltpu.VMEM((2, n_seq, PER, 2 * SUB, LANES), bf16),
            pltpu.VMEM((n_seq, PER, 2 * SUB, LANES), bf16),
            pltpu.VMEM((2 * rows, rows), bf16),
            pltpu.VMEM((2 * rows, rows), bf16),
            pltpu.VMEM((rows, 2 * rows), bf16),
            pltpu.VMEM((2, rows, LANES), f32),
            pltpu.VMEM((4, 2 * LANES, 2 * LANES), bf16),
            pltpu.VMEM((rows, 4 * LANES), bf16),
            pltpu.VMEM((PER, 2, rows, 2 * LANES), f32),
            pltpu.VMEM((2 * rows, 2 * LANES), bf16),
            pltpu.VMEM((2 * n_seq, PER, SUB, LANES), bf16),
            pltpu.VMEM((2, n_seq, PER, SUB, LANES), f32),
            pltpu.VMEM((n_seq, PER, SUB, LANES), f32),
            pltpu.VMEM((n_seq, PER, SUB, LANES), bf16),
            pltpu.SemaphoreType.DMA((4,)),
            pltpu.SemaphoreType.DMA((5,)),
            pltpu.SemaphoreType.DMA((6,)),
            pltpu.SemaphoreType.DMA((6,)),
        ],
        compiler_params=pltpu.CompilerParams(
            has_side_effects=True, vmem_limit_bytes=60 * 1024 * 1024
        ),
    )(z_input, gate_input, cotangent, spectrum, lengths, high, low, back, turn, inner)


def on_device(z_input, gate_input, cotangent, spectrum, skip_gain, lengths):
    n_seq = lax.axis_size("seq")
    span = z_input.shape[1]
    times = lax.axis_index("seq") * span + jnp.arange(span, dtype=jnp.int32)
    alive = (times < lengths[0])[:, None]
    s_rows, conv = mixer(n_seq, z_input, gate_input, cotangent, spectrum, lengths)
    product = cotangent[0].astype(jnp.float32) * gate_input[0].astype(jnp.float32)
    grad = product.astype(jnp.bfloat16).astype(jnp.float32)
    z_grad = jnp.where(alive, skip_gain * grad + conv.astype(jnp.float32), 0.0)
    return (z_grad.astype(jnp.bfloat16)[None], s_rows.astype(jnp.float32)[:, :, None])


def solution(mesh):
    return jax.shard_map(
        on_device,
        mesh=mesh,
        in_specs=(
            P("user", "seq", None),
            P("user", "seq", None),
            P("user", "seq", None),
            P(None, None, "seq", None, None),
            P(),
            P("user"),
        ),
        out_specs=(P("user", "seq", None), P(None, None, "seq", "user", None)),
        check_vma=False,
    )
```

```python
import functools

import jax
import jax.numpy as jnp
import ml_dtypes
import numpy as np
from jax import lax
from jax.experimental import pallas as pl
from jax.experimental.pallas import tpu as pltpu
from jax.sharding import PartitionSpec as P

LANES = 128
SUB = 8
PER = 3


def split_bf16(values):
    high = values.astype(ml_dtypes.bfloat16)
    low = (values - high.astype(np.float64)).astype(ml_dtypes.bfloat16)
    return high, low


def tables(n_seq):
    rows = SUB * n_seq
    total = rows * LANES
    index = np.arange(rows)
    freq = (index // SUB) + n_seq * (index % SUB)
    outer, turn = [], []
    for parity in range(2):
        twice = 2 * freq + parity
        angle = (twice[:, None] * index[None, :]) % (2 * rows) * (np.pi / rows)
        outer.append(np.concatenate([np.cos(angle), -np.sin(angle)], 0))
        small = twice[:, None] * np.arange(LANES)[None, :] * (np.pi / total)
        turn.append(np.stack([np.cos(small), -np.sin(small)]))
    outer = np.stack(outer)
    high, low = split_bf16(outer)
    back = np.ascontiguousarray(high.transpose(0, 2, 1))
    lane = np.arange(LANES)
    angle = (lane[:, None] * lane[None, :]) % LANES * (2 * np.pi / LANES)
    cos, sin = np.cos(angle), np.sin(angle)
    forward = np.block([[cos, -sin], [sin, cos]])
    inverse = np.block([[cos, sin], [-sin, cos]])
    fwd_high, fwd_low = split_bf16(forward)
    inv_high, inv_low = split_bf16(inverse)
    inner = np.stack([fwd_high, fwd_low, inv_high, inv_low])
    return high, low, back, np.stack(turn).astype(np.float32), inner


def visit(n_seq, place, bit, act):
    places = n_seq // 2
    planes = 8 if places % 8 == 0 else 1
    inner = places // planes

    def group(step, skip):
        for plane in range(planes):
            there = place + step + (plane * 3 % planes) * inner
            there = jnp.where(there >= places, there - places, there)
            if plane or not skip:
                act(there, bit)
            act(there, 1 - bit)

    group(0, True)

    def body(step, carry):
        group(step, False)
        return carry

    lax.fori_loop(1, inner, body, 0)


def kernel(
    n_seq,
    z_hbm,
    gate_hbm,
    cot_hbm,
    h_hbm,
    limit_ref,
    gain_ref,
    high_ref,
    low_ref,
    back_ref,
    turn_ref,
    inner_ref,
    s_final,
    z_final,
    z_in,
    gate_in,
    cot_in,
    h_in,
    stage,
    wide,
    zg_ref,
    h_ref,
    s_out,
    c_out,
    s_turned,
    z_turned,
    g_keep,
    zbuf,
    hbuf,
    m_high,
    m_low,
    m_back,
    m_turn,
    m_inner,
    x_buf,
    g_buf,
    b_buf,
    s_send,
    c_part,
    c_other,
    c_send,
    input_sems,
    table_sems,
    send_sems,
    recv_sems,
):
    rows = SUB * n_seq
    block = min(256, rows)
    groups = block // SUB
    blocks = rows // block
    scale = 1.0 / (2.0 * rows * LANES)
    seq = lax.axis_index("seq")
    user = lax.axis_index("user")
    core = lax.rem(seq, 2)
    place = seq // 2
    chip = place * 2 + user

    def remote(src, dst, which, device):
        return pltpu.make_async_remote_copy(
            src_ref=src,
            dst_ref=dst,
            send_sem=send_sems.at[which],
            recv_sem=recv_sems.at[which],
            device_id=device,
            device_id_type=pl.DeviceIdType.MESH,
        )

    def await_all(ref, sem):
        pltpu.make_async_copy(ref, ref, sem).wait()

    def await_sent(which, some):
        @pl.when(core == user)
        def _():
            await_all(some(n_seq - 1), send_sems.at[which])

        @pl.when(core != user)
        def _():
            await_all(some(n_seq), send_sems.at[which])

    inputs = [
        pltpu.make_async_copy(z_hbm.at[0], z_in, input_sems.at[0]),
        pltpu.make_async_copy(gate_hbm.at[0], gate_in, input_sems.at[1]),
        pltpu.make_async_copy(cot_hbm.at[0], cot_in, input_sems.at[2]),
        pltpu.make_async_copy(h_hbm.at[user, :, 0], h_in, input_sems.at[3]),
    ]
    loads = [
        pltpu.make_async_copy(high_ref.at[core], m_high, table_sems.at[0]),
        pltpu.make_async_copy(low_ref.at[core], m_low, table_sems.at[1]),
        pltpu.make_async_copy(back_ref.at[core], m_back, table_sems.at[2]),
        pltpu.make_async_copy(turn_ref.at[core], m_turn, table_sems.at[3]),
        pltpu.make_async_copy(inner_ref, m_inner, table_sems.at[4]),
    ]
    for load in inputs + loads:
        load.start()

    barrier = pltpu.get_barrier_semaphore()

    def greet(there, bit):
        pl.semaphore_signal(
            barrier,
            inc=1,
            device_id={"seq": 2 * there + bit, "user": core},
            device_id_type=pl.DeviceIdType.MESH,
        )

    @pl.when(core != user)
    def _():
        greet(place, core)

    visit(n_seq, place, core, greet)

    channels = PER * n_seq
    for load in inputs[:3]:
        load.wait()

    def pack(column, dst):
        size = n_seq * 2 * SUB // 4

        def body(part, carry):
            first = pl.multiple_of(column * n_seq * 2 * SUB + part * size, 8)
            tile = stage[pl.ds(first, size), :].reshape(n_seq // 4, 2 * SUB, LANES)
            dst[pl.ds(part * (n_seq // 4), n_seq // 4)] = tile.astype(jnp.bfloat16)
            return carry

        lax.fori_loop(0, 4, body, 0)

    def scatter(which, src, dst):
        def put(there, bit):
            to = {"seq": 2 * there + user, "user": bit}
            remote(src(2 * there + bit), dst, which, to).start()

        @pl.when(core == user)
        def _():
            pltpu.make_async_copy(src(chip), dst, recv_sems.at[which]).start()

        @pl.when(core != user)
        def _():
            put(place, user)

        visit(n_seq, place, user, put)

    def scatter_zg(which, columns):
        scatter(which, lambda target: zg_ref.at[columns, target], zbuf.at[user, columns, seq])

    first, others = pl.ds(0, 1), pl.ds(1, PER - 1)
    for column in range(PER):
        cut = slice(column * n_seq, (column + 1) * n_seq)

        def turn_zg(part, carry, column=column, cut=cut):
            at = pl.ds(pl.multiple_of(part * LANES, LANES), LANES)
            times = seq * (SUB * LANES) + part * LANES
            times = times + lax.broadcasted_iota(jnp.int32, (LANES, n_seq), 0)
            alive = times < limit_ref[0]
            z = jnp.where(alive, z_in[at, cut].astype(jnp.float32), 0.0)
            g = cot_in[at, cut].astype(jnp.float32) * gate_in[at, cut].astype(jnp.float32)
            g = jnp.where(alive, g, 0.0)
            g_keep[at, cut] = g.astype(jnp.bfloat16)
            top = column * n_seq * 2 * SUB + part
            stage[pl.ds(top, n_seq, stride=2 * SUB), :] = z.T
            stage[pl.ds(top + SUB, n_seq, stride=2 * SUB), :] = g.T
            return carry

        lax.fori_loop(0, SUB, turn_zg, 0)
        pack(column, zg_ref.at[column])
        if column == 0:

            @pl.when(core == user)
            def _():
                pl.semaphore_wait(barrier, n_seq - 1)

            @pl.when(core != user)
            def _():
                pl.semaphore_wait(barrier, n_seq)

            scatter_zg(0, first)
    scatter_zg(1, others)

    inputs[3].wait()
    for column in range(PER):
        cut = slice(column * n_seq, (column + 1) * n_seq)
        for kind in range(2):
            wide[kind, :, :n_seq] = h_in[kind, :, cut].astype(jnp.float32)

        def turn_h(low_bits, carry, column=column):
            for kind in range(2):
                tile = wide[kind, pl.ds(low_bits, LANES, stride=SUB), :]
                first = column * n_seq * 2 * SUB + kind * SUB + low_bits
                stage[pl.ds(first, n_seq, stride=2 * SUB), :] = tile.T[:n_seq]
            return carry

        lax.fori_loop(0, SUB, turn_h, 0)
        pack(column, h_ref.at[:, column])
    scatter(3, lambda target: h_ref.at[target], hbuf.at[seq])

    for load in loads:
        load.wait()

    mate = {"seq": seq + 1 - 2 * core, "user": user}

    def forward(channel, carry):
        for which, columns in ((0, first), (1, others)):

            @pl.when(channel == which)
            def _(which=which, columns=columns):
                arrived = zbuf.at[core, columns]
                await_all(arrived, recv_sems.at[which])
                swap = remote(arrived, arrived, 4 + which, mate)
                swap.start()
                swap.wait()

        def fill(part, inner_carry):
            for who in range(2):
                tile = zbuf[who, channel, pl.ds(part * groups, groups)]
                tile = tile.astype(jnp.float32)
                at = pl.ds(pl.multiple_of(part * block, block), block)
                for kind in range(2):
                    piece = tile[:, kind * SUB : (kind + 1) * SUB, :]
                    piece = piece.reshape(block, LANES).astype(jnp.bfloat16)
                    left = (2 * who + kind) * LANES
                    x_buf[at, left : left + LANES] = piece
            return inner_carry

        lax.fori_loop(0, blocks, fill, 0)

        def spectrum(part, inner_carry):
            start = pl.multiple_of(part * block, block)
            at = pl.ds(start, block)
            below = pl.ds(pl.multiple_of(rows + part * block, block), block)
            x = x_buf[...]
            dot = functools.partial(jnp.dot, preferred_element_type=jnp.float32)
            y_real = dot(m_high[at, :], x) + dot(m_low[at, :], x)
            y_imag = dot(m_high[below, :], x) + dot(m_low[below, :], x)
            t_real, t_imag = m_turn[0, at, :], m_turn[1, at, :]
            s_real = s_imag = None
            for who in range(2):
                spectra = []
                for kind in range(2):
                    left = (2 * who + kind) * LANES
                    a_real = y_real[:, left : left + LANES]
                    a_imag = y_imag[:, left : left + LANES]
                    mid = jnp.concatenate(
                        [a_real * t_real - a_imag * t_imag, a_real * t_imag + a_imag * t_real],
                        axis=1,
                    ).astype(jnp.bfloat16)
                    spectra.append(dot(mid, m_inner[0]) + dot(mid, m_inner[1]))
                z, g = spectra
                g_buf[channel, who, at, :] = g
                z_real, z_imag = z[:, :LANES], z[:, LANES:]
                g_real, g_imag = g[:, :LANES], g[:, LANES:]
                c_real = z_real * g_real + z_imag * g_imag
                c_imag = z_real * g_imag - z_imag * g_real
                s_real = c_real if who == 0 else s_real + c_real
                s_imag = c_imag if who == 0 else s_imag + c_imag
            s_real, s_imag = s_real * scale, s_imag * scale
            half = LANES // 2
            for who in range(2):
                cut = slice(who * half, (who + 1) * half)
                out = jnp.concatenate([s_real[:, cut], s_imag[:, cut]], axis=1)
                out = out.reshape(groups, SUB, LANES).astype(jnp.bfloat16)
                s_send[pl.ds(who * n_seq + part * groups, groups), channel] = out
            return inner_carry

        lax.fori_loop(0, blocks, spectrum, 0)
        return carry

    lax.fori_loop(0, PER, forward, 0)

    slot = core * n_seq + chip

    def put_s(there, bit, other):
        owner = 2 * there + other
        src = s_send.at[bit * n_seq + owner]
        remote(src, s_out.at[slot], 7, {"seq": owner, "user": bit}).start()

    def put_both(there, bit):
        put_s(there, bit, 0)
        put_s(there, bit, 1)

    pltpu.make_async_copy(s_send.at[user * n_seq + seq], s_out.at[slot], recv_sems.at[7]).start()
    put_s(place, user, 1 - core)
    visit(n_seq, place, user, put_both)

    await_all(hbuf, recv_sems.at[3])

    def inverse(channel, carry):
        dot = functools.partial(jnp.dot, preferred_element_type=jnp.float32)

        def product(part, inner_carry):
            at = pl.ds(pl.multiple_of(part * block, block), block)
            below = pl.ds(pl.multiple_of(rows + part * block, block), block)
            tile = hbuf[pl.ds(part * groups, groups), channel].astype(jnp.float32)
            h_real = tile[:, :SUB, :].reshape(block, LANES)
            h_imag = tile[:, SUB:, :].reshape(block, LANES)
            t_real, t_imag = m_turn[0, at, :], m_turn[1, at, :]
            for who in range(2):
                g = g_buf[channel, who, at, :]
                g_real, g_imag = g[:, :LANES], g[:, LANES:]
                q = jnp.concatenate(
                    [h_real * g_real + h_imag * g_imag, h_real * g_imag - h_imag * g_real],
                    axis=1,
                ).astype(jnp.bfloat16)
                b = dot(q, m_inner[2]) + dot(q, m_inner[3])
                b_real, b_imag = b[:, :LANES], b[:, LANES:]
                left = who * LANES
                b_buf[at, left : left + LANES] = (b_real * t_real + b_imag * t_imag).astype(
                    jnp.bfloat16
                )
                b_buf[below, left : left + LANES] = (b_imag * t_real - b_real * t_imag).astype(
                    jnp.bfloat16
                )
            return inner_carry

        lax.fori_loop(0, blocks, product, 0)

        def fold(part, inner_carry):
            at = pl.ds(pl.multiple_of(part * block, block), block)
            conv = dot(m_back[at, :], b_buf[...]) * scale
            for who in range(2):
                piece = conv[:, who * LANES : (who + 1) * LANES]
                c_part[who, pl.ds(part * groups, groups), channel] = piece.reshape(
                    groups, SUB, LANES
                )
            return inner_carry

        lax.fori_loop(0, blocks, fold, 0)
        return carry

    lax.fori_loop(0, PER, inverse, 0)

    swap_back = remote(c_part.at[1 - core], c_other, 8, mate)
    swap_back.start()
    swap_back.wait()

    def join(part, carry):
        at = pl.ds(part * groups, groups)
        c_send[at] = (c_part[core, at] + c_other[at]).astype(jnp.bfloat16)
        return carry

    lax.fori_loop(0, blocks, join, 0)

    def put_c(there, bit):
        target = 2 * there + bit
        remote(c_send.at[target], c_out.at[chip], 9, {"seq": target, "user": core}).start()

    @pl.when(core == user)
    def _():
        pltpu.make_async_copy(c_send.at[seq], c_out.at[chip], recv_sems.at[9]).start()

    @pl.when(core != user)
    def _():
        put_c(place, core)

    visit(n_seq, place, core, put_c)

    def unpack(column, src):
        size = n_seq * SUB // 4

        def body(part, carry):
            tile = src[pl.ds(part * (n_seq // 4), n_seq // 4)].astype(jnp.float32)
            first = pl.multiple_of(column * n_seq * SUB + part * size, 8)
            stage[pl.ds(first, size), :] = tile.reshape(size, LANES)
            return carry

        lax.fori_loop(0, 4, body, 0)

    half = LANES // 2
    await_all(s_out, recv_sems.at[7])
    for parity in range(2):
        for column in range(PER):
            cut = slice(column * n_seq, (column + 1) * n_seq)
            unpack(column, s_out.at[pl.ds(parity * n_seq, n_seq), column])

            def turn_s(low_bits, carry, column=column):
                first = column * n_seq * SUB + low_bits
                tile = stage[pl.ds(first, n_seq, stride=SUB), :].T
                for kind in range(2):
                    piece = tile[kind * half : (kind + 1) * half]
                    first = kind * half * SUB + low_bits
                    wide[column, pl.ds(first, half, stride=SUB), :n_seq] = piece
                return carry

            lax.fori_loop(0, SUB, turn_s, 0)
            for kind in range(2):
                at = pl.ds(kind * half * SUB, half * SUB)
                s_turned[parity, kind, :, cut] = wide[column, at, :n_seq].astype(jnp.bfloat16)
    s_store = pltpu.make_async_copy(s_turned, s_final, input_sems.at[0])
    s_store.start()

    await_all(c_out, recv_sems.at[9])
    for column in range(PER):
        unpack(column, c_out.at[:, column])

    def finish(part, carry):
        at = pl.ds(pl.multiple_of(part * LANES, LANES), LANES)
        times = seq * (SUB * LANES) + part * LANES
        times = times + lax.broadcasted_iota(jnp.int32, (LANES, n_seq), 0)
        alive = times < limit_ref[0]
        for column in range(PER):
            cut = slice(column * n_seq, (column + 1) * n_seq)
            conv = stage[pl.ds(column * n_seq * SUB + part, n_seq, stride=SUB), :].T
            total = gain_ref[:, cut] * g_keep[at, cut].astype(jnp.float32) + conv
            z_turned[at, cut] = jnp.where(alive, total, 0.0).astype(jnp.bfloat16)
        return carry

    lax.fori_loop(0, SUB, finish, 0)
    z_store = pltpu.make_async_copy(z_turned, z_final.at[0], input_sems.at[1])
    z_store.start()

    await_sent(0, lambda count: zg_ref.at[first, pl.ds(0, count)])
    await_sent(1, lambda count: zg_ref.at[others, pl.ds(0, count)])
    await_sent(3, lambda count: h_ref.at[pl.ds(0, count)])
    await_all(s_send.at[pl.ds(0, 2 * n_seq - 1)], send_sems.at[7])
    await_sent(9, lambda count: c_send.at[pl.ds(0, count)])
    s_store.wait()
    z_store.wait()


def mixer(n_seq, z_input, gate_input, cotangent, spectrum, skip_gain, lengths):
    rows = SUB * n_seq
    span, channels = z_input.shape[1:]
    bf16, f32 = jnp.bfloat16, jnp.float32
    high, low, back, turn, inner = (jnp.asarray(t) for t in tables(n_seq))
    gain = skip_gain.reshape(1, channels)
    anywhere = pl.BlockSpec(memory_space=pl.ANY)
    return pl.pallas_call(
        functools.partial(kernel, n_seq),
        out_shape=(
            jax.ShapeDtypeStruct((2, 2, span // 2, channels), bf16),
            jax.ShapeDtypeStruct((1, span, channels), bf16),
        ),
        in_specs=[anywhere] * 4
        + [pl.BlockSpec(memory_space=pltpu.SMEM), pl.BlockSpec(memory_space=pltpu.VMEM)]
        + [anywhere] * 5,
        out_specs=(anywhere, anywhere),
        scratch_shapes=[
            pltpu.VMEM((span, channels), bf16),
            pltpu.VMEM((span, channels), bf16),
            pltpu.VMEM((span, channels), bf16),
            pltpu.VMEM((2, span, channels), bf16),
            pltpu.VMEM((channels * 2 * SUB, LANES), f32),
            pltpu.VMEM((PER, span, LANES), f32),
            pltpu.VMEM((PER, n_seq, 2 * SUB, LANES), bf16),
            pltpu.VMEM((n_seq, PER, 2 * SUB, LANES), bf16),
            pltpu.VMEM((2 * n_seq, PER, SUB, LANES), bf16),
            pltpu.VMEM((n_seq, PER, SUB, LANES), bf16),
            pltpu.VMEM((2, 2, span // 2, channels), bf16),
            pltpu.VMEM((span, channels), bf16),
            pltpu.VMEM((span, channels), bf16),
            pltpu.VMEM((2, PER, n_seq, 2 * SUB, LANES), bf16),
            pltpu.VMEM((n_seq, PER, 2 * SUB, LANES), bf16),
            pltpu.VMEM((2 * rows, rows), bf16),
            pltpu.VMEM((2 * rows, rows), bf16),
            pltpu.VMEM((rows, 2 * rows), bf16),
            pltpu.VMEM((2, rows, LANES), f32),
            pltpu.VMEM((4, 2 * LANES, 2 * LANES), bf16),
            pltpu.VMEM((rows, 4 * LANES), bf16),
            pltpu.VMEM((PER, 2, rows, 2 * LANES), f32),
            pltpu.VMEM((2 * rows, 2 * LANES), bf16),
            pltpu.VMEM((2 * n_seq, PER, SUB, LANES), bf16),
            pltpu.VMEM((2, n_seq, PER, SUB, LANES), f32),
            pltpu.VMEM((n_seq, PER, SUB, LANES), f32),
            pltpu.VMEM((n_seq, PER, SUB, LANES), bf16),
            pltpu.SemaphoreType.DMA((4,)),
            pltpu.SemaphoreType.DMA((5,)),
            pltpu.SemaphoreType.DMA((10,)),
            pltpu.SemaphoreType.DMA((10,)),
        ],
        compiler_params=pltpu.CompilerParams(
            collective_id=0, has_side_effects=True, vmem_limit_bytes=60 * 1024 * 1024
        ),
    )(z_input, gate_input, cotangent, spectrum, lengths, gain, high, low, back, turn, inner)


def on_device(z_input, gate_input, cotangent, spectrum, skip_gain, lengths):
    n_seq = lax.axis_size("seq")
    s_rows, z_grad = mixer(
        n_seq, z_input, gate_input, cotangent, spectrum, skip_gain, lengths
    )
    return (z_grad, s_rows.astype(jnp.float32)[:, :, None])


def solution(mesh):
    return jax.shard_map(
        on_device,
        mesh=mesh,
        in_specs=(
            P("user", "seq", None),
            P("user", "seq", None),
            P("user", "seq", None),
            P(None, None, "seq", None, None),
            P(),
            P("user"),
        ),
        out_specs=(P("user", "seq", None), P(None, None, "seq", "user", None)),
        check_vma=False,
    )
```

```python
import functools

import jax
import jax.numpy as jnp
import ml_dtypes
import numpy as np
from jax import lax
from jax.experimental import pallas as pl
from jax.experimental.pallas import tpu as pltpu
from jax.sharding import PartitionSpec as P

LANES = 128
SUB = 8
PER = 3


def split_bf16(values):
    high = values.astype(ml_dtypes.bfloat16)
    low = (values - high.astype(np.float64)).astype(ml_dtypes.bfloat16)
    return high, low


def tables(n_seq):
    rows = SUB * n_seq
    total = rows * LANES
    index = np.arange(rows)
    freq = (index // SUB) + n_seq * (index % SUB)
    outer, turn = [], []
    for parity in range(2):
        twice = 2 * freq + parity
        angle = (twice[:, None] * index[None, :]) % (2 * rows) * (np.pi / rows)
        outer.append(np.concatenate([np.cos(angle), -np.sin(angle)], 0))
        small = twice[:, None] * np.arange(LANES)[None, :] * (np.pi / total)
        turn.append(np.stack([np.cos(small), -np.sin(small)]))
    outer = np.stack(outer)
    high, low = split_bf16(outer)
    back = np.ascontiguousarray(high.transpose(0, 2, 1))
    lane = np.arange(LANES)
    angle = (lane[:, None] * lane[None, :]) % LANES * (2 * np.pi / LANES)
    cos, sin = np.cos(angle), np.sin(angle)
    forward = np.block([[cos, -sin], [sin, cos]])
    inverse = np.block([[cos, sin], [-sin, cos]])
    fwd_high, fwd_low = split_bf16(forward)
    inv_high, inv_low = split_bf16(inverse)
    inner = np.stack([fwd_high, fwd_low, inv_high, inv_low])
    return high, low, back, np.stack(turn).astype(np.float32), inner


def visit(n_seq, place, bit, act):
    places = n_seq // 2
    planes = 8 if places % 8 == 0 else 1
    inner = places // planes

    def group(step, skip):
        for plane in range(planes):
            there = place + step + (plane * 3 % planes) * inner
            there = jnp.where(there >= places, there - places, there)
            if plane or not skip:
                act(there, bit)
            act(there, 1 - bit)

    group(0, True)

    def body(step, carry):
        group(step, False)
        return carry

    lax.fori_loop(1, inner, body, 0)


def kernel(
    n_seq,
    z_hbm,
    gate_hbm,
    cot_hbm,
    h_hbm,
    limit_ref,
    gain_ref,
    high_ref,
    low_ref,
    back_ref,
    turn_ref,
    inner_ref,
    s_final,
    z_final,
    z_in,
    gate_in,
    cot_in,
    h_in,
    stage,
    wide,
    zg_ref,
    h_ref,
    s_out,
    c_out,
    g_keep,
    zbuf,
    hbuf,
    m_high,
    m_low,
    m_back,
    m_turn,
    m_inner,
    x_buf,
    g_buf,
    b_buf,
    s_send,
    s_cross,
    c_part,
    c_other,
    c_send,
    input_sems,
    table_sems,
    send_sems,
    recv_sems,
):
    rows = SUB * n_seq
    block = min(256, rows)
    groups = block // SUB
    blocks = rows // block
    scale = 1.0 / (2.0 * rows * LANES)
    seq = lax.axis_index("seq")
    user = lax.axis_index("user")
    core = lax.rem(seq, 2)
    place = seq // 2
    chip = place * 2 + user

    def remote(src, dst, which, device):
        return pltpu.make_async_remote_copy(
            src_ref=src,
            dst_ref=dst,
            send_sem=send_sems.at[which],
            recv_sem=recv_sems.at[which],
            device_id=device,
            device_id_type=pl.DeviceIdType.MESH,
        )

    def await_all(ref, sem):
        pltpu.make_async_copy(ref, ref, sem).wait()

    def await_sent(which, some):
        @pl.when(core == user)
        def _():
            await_all(some(n_seq - 1), send_sems.at[which])

        @pl.when(core != user)
        def _():
            await_all(some(n_seq), send_sems.at[which])

    inputs = [
        pltpu.make_async_copy(z_hbm.at[0], z_in, input_sems.at[0]),
        pltpu.make_async_copy(gate_hbm.at[0], gate_in, input_sems.at[1]),
        pltpu.make_async_copy(cot_hbm.at[0], cot_in, input_sems.at[2]),
        pltpu.make_async_copy(h_hbm.at[user, :, 0], h_in, input_sems.at[3]),
    ]
    loads = [
        pltpu.make_async_copy(high_ref.at[core], m_high, table_sems.at[0]),
        pltpu.make_async_copy(low_ref.at[core], m_low, table_sems.at[1]),
        pltpu.make_async_copy(back_ref.at[core], m_back, table_sems.at[2]),
        pltpu.make_async_copy(turn_ref.at[core], m_turn, table_sems.at[3]),
        pltpu.make_async_copy(inner_ref, m_inner, table_sems.at[4]),
    ]
    for load in inputs + loads:
        load.start()

    barrier = pltpu.get_barrier_semaphore()

    def greet(there, bit):
        pl.semaphore_signal(
            barrier,
            inc=1,
            device_id={"seq": 2 * there + bit, "user": core},
            device_id_type=pl.DeviceIdType.MESH,
        )

    @pl.when(core != user)
    def _():
        greet(place, core)

    visit(n_seq, place, core, greet)

    channels = PER * n_seq
    for load in inputs[:3]:
        load.wait()

    def pack(column, dst):
        size = n_seq * 2 * SUB // 4

        def body(part, carry):
            first = pl.multiple_of(column * n_seq * 2 * SUB + part * size, 8)
            tile = stage[pl.ds(first, size), :].reshape(n_seq // 4, 2 * SUB, LANES)
            dst[pl.ds(part * (n_seq // 4), n_seq // 4)] = tile.astype(jnp.bfloat16)
            return carry

        lax.fori_loop(0, 4, body, 0)

    def scatter(which, src, dst):
        def put(there, bit):
            to = {"seq": 2 * there + user, "user": bit}
            remote(src(2 * there + bit), dst, which, to).start()

        @pl.when(core == user)
        def _():
            pltpu.make_async_copy(src(chip), dst, recv_sems.at[which]).start()

        @pl.when(core != user)
        def _():
            put(place, user)

        visit(n_seq, place, user, put)

    for column in range(PER):
        cut = slice(column * n_seq, (column + 1) * n_seq)

        def turn_zg(part, carry, column=column, cut=cut):
            at = pl.ds(pl.multiple_of(part * LANES, LANES), LANES)
            times = seq * (SUB * LANES) + part * LANES
            times = times + lax.broadcasted_iota(jnp.int32, (LANES, n_seq), 0)
            alive = times < limit_ref[0]
            z = jnp.where(alive, z_in[at, cut].astype(jnp.float32), 0.0)
            g = cot_in[at, cut].astype(jnp.float32) * gate_in[at, cut].astype(jnp.float32)
            g = jnp.where(alive, g, 0.0)
            g_keep[at, cut] = g.astype(jnp.bfloat16)
            top = column * n_seq * 2 * SUB + part
            stage[pl.ds(top, n_seq, stride=2 * SUB), :] = z.T
            stage[pl.ds(top + SUB, n_seq, stride=2 * SUB), :] = g.T
            return carry

        lax.fori_loop(0, SUB, turn_zg, 0)
        pack(column, zg_ref.at[:, column])

    @pl.when(core == user)
    def _():
        pl.semaphore_wait(barrier, n_seq - 1)

    @pl.when(core != user)
    def _():
        pl.semaphore_wait(barrier, n_seq)

    scatter(0, lambda target: zg_ref.at[target], zbuf.at[user, seq])

    inputs[3].wait()
    for column in range(PER):
        cut = slice(column * n_seq, (column + 1) * n_seq)
        for kind in range(2):
            wide[kind, :, :n_seq] = h_in[kind, :, cut].astype(jnp.float32)

        def turn_h(low_bits, carry, column=column):
            for kind in range(2):
                tile = wide[kind, pl.ds(low_bits, LANES, stride=SUB), :]
                first = column * n_seq * 2 * SUB + kind * SUB + low_bits
                stage[pl.ds(first, n_seq, stride=2 * SUB), :] = tile.T[:n_seq]
            return carry

        lax.fori_loop(0, SUB, turn_h, 0)
        pack(column, h_ref.at[:, column])
    scatter(3, lambda target: h_ref.at[target], hbuf.at[seq])

    for load in loads:
        load.wait()

    mate = {"seq": seq + 1 - 2 * core, "user": user}

    arrived = zbuf.at[core]
    await_all(arrived, recv_sems.at[0])
    swap = remote(arrived, arrived, 1, mate)
    swap.start()
    swap.wait()

    def cross(channel):
        return remote(s_cross.at[channel], s_send.at[:, core, channel], 4 + channel, mate)

    def forward(channel, carry):
        def fill(part, inner_carry):
            for who in range(2):
                tile = zbuf[who, pl.ds(part * groups, groups), channel]
                tile = tile.astype(jnp.float32)
                at = pl.ds(pl.multiple_of(part * block, block), block)
                for kind in range(2):
                    piece = tile[:, kind * SUB : (kind + 1) * SUB, :]
                    piece = piece.reshape(block, LANES).astype(jnp.bfloat16)
                    left = (2 * who + kind) * LANES
                    x_buf[at, left : left + LANES] = piece
            return inner_carry

        lax.fori_loop(0, blocks, fill, 0)

        def spectrum(part, inner_carry):
            start = pl.multiple_of(part * block, block)
            at = pl.ds(start, block)
            below = pl.ds(pl.multiple_of(rows + part * block, block), block)
            x = x_buf[...]
            dot = functools.partial(jnp.dot, preferred_element_type=jnp.float32)
            y_real = dot(m_high[at, :], x) + dot(m_low[at, :], x)
            y_imag = dot(m_high[below, :], x) + dot(m_low[below, :], x)
            t_real, t_imag = m_turn[0, at, :], m_turn[1, at, :]
            s_real = s_imag = None
            for who in range(2):
                spectra = []
                for kind in range(2):
                    left = (2 * who + kind) * LANES
                    a_real = y_real[:, left : left + LANES]
                    a_imag = y_imag[:, left : left + LANES]
                    mid = jnp.concatenate(
                        [a_real * t_real - a_imag * t_imag, a_real * t_imag + a_imag * t_real],
                        axis=1,
                    ).astype(jnp.bfloat16)
                    spectra.append(dot(mid, m_inner[0]) + dot(mid, m_inner[1]))
                z, g = spectra
                g_buf[channel, who, at, :] = g
                z_real, z_imag = z[:, :LANES], z[:, LANES:]
                g_real, g_imag = g[:, :LANES], g[:, LANES:]
                c_real = z_real * g_real + z_imag * g_imag
                c_imag = z_real * g_imag - z_imag * g_real
                s_real = c_real if who == 0 else s_real + c_real
                s_imag = c_imag if who == 0 else s_imag + c_imag
            s_real, s_imag = s_real * scale, s_imag * scale
            half = LANES // 2
            outs = []
            for who in range(2):
                cut = slice(who * half, (who + 1) * half)
                out = jnp.concatenate([s_real[:, cut], s_imag[:, cut]], axis=1)
                outs.append(out.reshape(groups, SUB, LANES))
            here = pl.ds(part * groups, groups)
            s_send[here, core, channel] = jnp.where(core == 0, outs[0], outs[1]).astype(jnp.bfloat16)
            s_cross[channel, here] = jnp.where(core == 0, outs[1], outs[0]).astype(jnp.bfloat16)
            return inner_carry

        lax.fori_loop(0, blocks, spectrum, 0)
        cross(channel).start()
        return carry

    lax.fori_loop(0, PER, forward, 0)

    for channel in range(PER):
        cross(channel).wait()

    def gather(which, src, dst):
        def put(there, bit):
            to = {"seq": 2 * there + bit, "user": core}
            remote(src.at[2 * there + bit], dst.at[chip], which, to).start()

        @pl.when(core == user)
        def _():
            pltpu.make_async_copy(src.at[seq], dst.at[chip], recv_sems.at[which]).start()

        @pl.when(core != user)
        def _():
            put(place, core)

        visit(n_seq, place, core, put)

    gather(7, s_send, s_out)

    await_all(hbuf, recv_sems.at[3])

    def inverse(channel, carry):
        dot = functools.partial(jnp.dot, preferred_element_type=jnp.float32)

        def product(part, inner_carry):
            at = pl.ds(pl.multiple_of(part * block, block), block)
            below = pl.ds(pl.multiple_of(rows + part * block, block), block)
            tile = hbuf[pl.ds(part * groups, groups), channel].astype(jnp.float32)
            h_real = tile[:, :SUB, :].reshape(block, LANES)
            h_imag = tile[:, SUB:, :].reshape(block, LANES)
            t_real, t_imag = m_turn[0, at, :], m_turn[1, at, :]
            for who in range(2):
                g = g_buf[channel, who, at, :]
                g_real, g_imag = g[:, :LANES], g[:, LANES:]
                q = jnp.concatenate(
                    [h_real * g_real + h_imag * g_imag, h_real * g_imag - h_imag * g_real],
                    axis=1,
                ).astype(jnp.bfloat16)
                b = dot(q, m_inner[2]) + dot(q, m_inner[3])
                b_real, b_imag = b[:, :LANES], b[:, LANES:]
                left = who * LANES
                b_buf[at, left : left + LANES] = (b_real * t_real + b_imag * t_imag).astype(
                    jnp.bfloat16
                )
                b_buf[below, left : left + LANES] = (b_imag * t_real - b_real * t_imag).astype(
                    jnp.bfloat16
                )
            return inner_carry

        lax.fori_loop(0, blocks, product, 0)

        def fold(part, inner_carry):
            at = pl.ds(pl.multiple_of(part * block, block), block)
            conv = dot(m_back[at, :], b_buf[...]) * scale
            for who in range(2):
                piece = conv[:, who * LANES : (who + 1) * LANES]
                c_part[who, pl.ds(part * groups, groups), channel] = piece.reshape(
                    groups, SUB, LANES
                )
            return inner_carry

        lax.fori_loop(0, blocks, fold, 0)
        return carry

    lax.fori_loop(0, PER, inverse, 0)

    swap_back = remote(c_part.at[1 - core], c_other, 8, mate)
    swap_back.start()
    swap_back.wait()

    def join(part, carry):
        at = pl.ds(part * groups, groups)
        c_send[at] = (c_part[core, at] + c_other[at]).astype(jnp.bfloat16)
        return carry

    lax.fori_loop(0, blocks, join, 0)

    gather(9, c_send, c_out)

    def unpack(column, src):
        size = n_seq * SUB // 4

        def body(part, carry):
            tile = src[pl.ds(part * (n_seq // 4), n_seq // 4)].astype(jnp.float32)
            first = pl.multiple_of(column * n_seq * SUB + part * size, 8)
            stage[pl.ds(first, size), :] = tile.reshape(size, LANES)
            return carry

        lax.fori_loop(0, 4, body, 0)

    half = LANES // 2
    await_all(s_out, recv_sems.at[7])
    for parity in range(2):
        for column in range(PER):
            cut = slice(column * n_seq, (column + 1) * n_seq)
            unpack(column, s_out.at[:, parity, column])

            def turn_s(low_bits, carry, column=column):
                first = column * n_seq * SUB + low_bits
                tile = stage[pl.ds(first, n_seq, stride=SUB), :].T
                for kind in range(2):
                    piece = tile[kind * half : (kind + 1) * half]
                    first = kind * half * SUB + low_bits
                    wide[column, pl.ds(first, half, stride=SUB), :n_seq] = piece
                return carry

            lax.fori_loop(0, SUB, turn_s, 0)
            for kind in range(2):
                at = pl.ds(kind * half * SUB, half * SUB)
                s_final[parity, kind, :, cut] = wide[column, at, :n_seq].astype(jnp.bfloat16)

    await_all(c_out, recv_sems.at[9])
    for column in range(PER):
        unpack(column, c_out.at[:, column])

    def finish(part, carry):
        at = pl.ds(pl.multiple_of(part * LANES, LANES), LANES)
        times = seq * (SUB * LANES) + part * LANES
        times = times + lax.broadcasted_iota(jnp.int32, (LANES, n_seq), 0)
        alive = times < limit_ref[0]
        for column in range(PER):
            cut = slice(column * n_seq, (column + 1) * n_seq)
            conv = stage[pl.ds(column * n_seq * SUB + part, n_seq, stride=SUB), :].T
            total = gain_ref[cut][None, :] * g_keep[at, cut].astype(jnp.float32) + conv
            z_final[0, at, cut] = jnp.where(alive, total, 0.0).astype(jnp.bfloat16)
        return carry

    lax.fori_loop(0, SUB, finish, 0)

    await_sent(0, lambda count: zg_ref.at[pl.ds(0, count)])
    await_sent(3, lambda count: h_ref.at[pl.ds(0, count)])
    await_sent(7, lambda count: s_send.at[pl.ds(0, count)])
    await_sent(9, lambda count: c_send.at[pl.ds(0, count)])


def mixer(n_seq, z_input, gate_input, cotangent, spectrum, skip_gain, lengths):
    rows = SUB * n_seq
    span, channels = z_input.shape[1:]
    bf16, f32 = jnp.bfloat16, jnp.float32
    high, low, back, turn, inner = (jnp.asarray(t) for t in tables(n_seq))
    anywhere = pl.BlockSpec(memory_space=pl.ANY)
    return pl.pallas_call(
        functools.partial(kernel, n_seq),
        out_shape=(
            pltpu.VMEM((2, 2, span // 2, channels), bf16),
            pltpu.VMEM((1, span, channels), bf16),
        ),
        in_specs=[anywhere] * 4
        + [pl.BlockSpec(memory_space=pltpu.SMEM), pl.BlockSpec(memory_space=pltpu.VMEM)]
        + [anywhere] * 5,
        out_specs=(pl.BlockSpec(memory_space=pltpu.VMEM),) * 2,
        scratch_shapes=[
            pltpu.VMEM((span, channels), bf16),
            pltpu.VMEM((span, channels), bf16),
            pltpu.VMEM((span, channels), bf16),
            pltpu.VMEM((2, span, channels), bf16),
            pltpu.VMEM((channels * 2 * SUB, LANES), f32),
            pltpu.VMEM((PER, span, LANES), f32),
            pltpu.VMEM((n_seq, PER, 2 * SUB, LANES), bf16),
            pltpu.VMEM((n_seq, PER, 2 * SUB, LANES), bf16),
            pltpu.VMEM((n_seq, 2, PER, SUB, LANES), bf16),
            pltpu.VMEM((n_seq, PER, SUB, LANES), bf16),
            pltpu.VMEM((span, channels), bf16),
            pltpu.VMEM((2, n_seq, PER, 2 * SUB, LANES), bf16),
            pltpu.VMEM((n_seq, PER, 2 * SUB, LANES), bf16),
            pltpu.VMEM((2 * rows, rows), bf16),
            pltpu.VMEM((2 * rows, rows), bf16),
            pltpu.VMEM((rows, 2 * rows), bf16),
            pltpu.VMEM((2, rows, LANES), f32),
            pltpu.VMEM((4, 2 * LANES, 2 * LANES), bf16),
            pltpu.VMEM((rows, 4 * LANES), bf16),
            pltpu.VMEM((PER, 2, rows, 2 * LANES), f32),
            pltpu.VMEM((2 * rows, 2 * LANES), bf16),
            pltpu.VMEM((n_seq, 2, PER, SUB, LANES), bf16),
            pltpu.VMEM((PER, n_seq, SUB, LANES), bf16),
            pltpu.VMEM((2, n_seq, PER, SUB, LANES), f32),
            pltpu.VMEM((n_seq, PER, SUB, LANES), f32),
            pltpu.VMEM((n_seq, PER, SUB, LANES), bf16),
            pltpu.SemaphoreType.DMA((4,)),
            pltpu.SemaphoreType.DMA((5,)),
            pltpu.SemaphoreType.DMA((10,)),
            pltpu.SemaphoreType.DMA((10,)),
        ],
        compiler_params=pltpu.CompilerParams(
            collective_id=0, has_side_effects=True, vmem_limit_bytes=56 * 1024 * 1024
        ),
    )(z_input, gate_input, cotangent, spectrum, lengths, skip_gain, high, low, back, turn, inner)


def on_device(z_input, gate_input, cotangent, spectrum, skip_gain, lengths):
    n_seq = lax.axis_size("seq")
    s_rows, z_grad = mixer(
        n_seq, z_input, gate_input, cotangent, spectrum, skip_gain, lengths
    )
    return (z_grad, s_rows.astype(jnp.float32)[:, :, None])


def solution(mesh):
    return jax.shard_map(
        on_device,
        mesh=mesh,
        in_specs=(
            P("user", "seq", None),
            P("user", "seq", None),
            P("user", "seq", None),
            P(None, None, "seq", None, None),
            P(),
            P("user"),
        ),
        out_specs=(P("user", "seq", None), P(None, None, "seq", "user", None)),
        check_vma=False,
    )
```

```python
import functools

import jax
import jax.numpy as jnp
import ml_dtypes
import numpy as np
from jax import lax
from jax.experimental import pallas as pl
from jax.experimental.pallas import tpu as pltpu
from jax.sharding import PartitionSpec as P

LANES = 128
SUB = 8
PER = 3


def split_bf16(values):
    high = values.astype(ml_dtypes.bfloat16)
    low = (values - high.astype(np.float64)).astype(ml_dtypes.bfloat16)
    return high, low


def tables(n_seq):
    rows = SUB * n_seq
    total = rows * LANES
    index = np.arange(rows)
    freq = (index // SUB) + n_seq * (index % SUB)
    outer, turn = [], []
    for parity in range(2):
        twice = 2 * freq + parity
        angle = (twice[:, None] * index[None, :]) % (2 * rows) * (np.pi / rows)
        outer.append(np.concatenate([np.cos(angle), -np.sin(angle)], 0))
        small = twice[:, None] * np.arange(LANES)[None, :] * (np.pi / total)
        turn.append(np.stack([np.cos(small), -np.sin(small)]))
    outer = np.stack(outer)
    high, low = split_bf16(outer)
    back = np.ascontiguousarray(high.transpose(0, 2, 1))
    lane = np.arange(LANES)
    angle = (lane[:, None] * lane[None, :]) % LANES * (2 * np.pi / LANES)
    cos, sin = np.cos(angle), np.sin(angle)
    forward = np.block([[cos, -sin], [sin, cos]])
    inverse = np.block([[cos, sin], [-sin, cos]])
    fwd_high, fwd_low = split_bf16(forward)
    inv_high, inv_low = split_bf16(inverse)
    inner = np.stack([fwd_high, fwd_low, inv_high, inv_low])
    return high, low, back, np.stack(turn).astype(np.float32), inner


def visit(n_seq, place, bit, act):
    places = n_seq // 2
    planes = 8 if places % 8 == 0 else 1
    inner = places // planes

    def group(step, skip):
        for plane in range(planes):
            there = place + step + (plane * 3 % planes) * inner
            there = jnp.where(there >= places, there - places, there)
            if plane or not skip:
                act(there, bit)
            act(there, 1 - bit)

    group(0, True)

    def body(step, carry):
        group(step, False)
        return carry

    lax.fori_loop(1, inner, body, 0)


def kernel(
    n_seq,
    z_hbm,
    gate_hbm,
    cot_hbm,
    h_hbm,
    limit_ref,
    gain_ref,
    high_ref,
    low_ref,
    back_ref,
    turn_ref,
    inner_ref,
    s_final,
    z_final,
    z_in,
    gate_in,
    cot_in,
    h_in,
    stage,
    wide,
    zg_ref,
    h_ref,
    s_out,
    c_out,
    g_keep,
    zbuf,
    hbuf,
    m_high,
    m_low,
    m_back,
    m_turn,
    m_inner,
    x_buf,
    g_buf,
    b_buf,
    s_send,
    s_cross,
    c_part,
    c_other,
    c_send,
    input_sems,
    table_sems,
    send_sems,
    recv_sems,
):
    rows = SUB * n_seq
    block = min(256, rows)
    groups = block // SUB
    blocks = rows // block
    scale = 1.0 / (2.0 * rows * LANES)
    seq = lax.axis_index("seq")
    user = lax.axis_index("user")
    core = lax.rem(seq, 2)
    place = seq // 2
    chip = place * 2 + user

    def remote(src, dst, which, device):
        return pltpu.make_async_remote_copy(
            src_ref=src,
            dst_ref=dst,
            send_sem=send_sems.at[which],
            recv_sem=recv_sems.at[which],
            device_id=device,
            device_id_type=pl.DeviceIdType.MESH,
        )

    def await_all(ref, sem):
        pltpu.make_async_copy(ref, ref, sem).wait()

    def await_sent(which, some):
        @pl.when(core == user)
        def _():
            await_all(some(n_seq - 1), send_sems.at[which])

        @pl.when(core != user)
        def _():
            await_all(some(n_seq), send_sems.at[which])

    inputs = [
        pltpu.make_async_copy(z_hbm.at[0], z_in, input_sems.at[0]),
        pltpu.make_async_copy(gate_hbm.at[0], gate_in, input_sems.at[1]),
        pltpu.make_async_copy(cot_hbm.at[0], cot_in, input_sems.at[2]),
        pltpu.make_async_copy(h_hbm.at[user, :, 0], h_in, input_sems.at[3]),
    ]
    loads = [
        pltpu.make_async_copy(high_ref.at[core], m_high, table_sems.at[0]),
        pltpu.make_async_copy(low_ref.at[core], m_low, table_sems.at[1]),
        pltpu.make_async_copy(back_ref.at[core], m_back, table_sems.at[2]),
        pltpu.make_async_copy(turn_ref.at[core], m_turn, table_sems.at[3]),
        pltpu.make_async_copy(inner_ref, m_inner, table_sems.at[4]),
    ]
    for load in inputs[:3]:
        load.start()

    barrier = pltpu.get_barrier_semaphore()

    def greet(there, bit):
        pl.semaphore_signal(
            barrier,
            inc=1,
            device_id={"seq": 2 * there + bit, "user": core},
            device_id_type=pl.DeviceIdType.MESH,
        )

    @pl.when(core != user)
    def _():
        greet(place, core)

    visit(n_seq, place, core, greet)
    for load in inputs[3:] + loads:
        load.start()

    channels = PER * n_seq
    for load in inputs[:3]:
        load.wait()

    def pack(column, dst):
        size = n_seq * 2 * SUB // 4

        def body(part, carry):
            first = pl.multiple_of(column * n_seq * 2 * SUB + part * size, 8)
            tile = stage[pl.ds(first, size), :].reshape(n_seq // 4, 2 * SUB, LANES)
            dst[pl.ds(part * (n_seq // 4), n_seq // 4)] = tile.astype(jnp.bfloat16)
            return carry

        lax.fori_loop(0, 4, body, 0)

    def scatter(which, src, dst):
        def put(there, bit):
            to = {"seq": 2 * there + user, "user": bit}
            remote(src(2 * there + bit), dst, which, to).start()

        @pl.when(core == user)
        def _():
            pltpu.make_async_copy(src(chip), dst, recv_sems.at[which]).start()

        @pl.when(core != user)
        def _():
            put(place, user)

        visit(n_seq, place, user, put)

    for column in range(PER):
        cut = slice(column * n_seq, (column + 1) * n_seq)

        def turn_zg(part, carry, column=column, cut=cut):
            at = pl.ds(pl.multiple_of(part * LANES, LANES), LANES)
            times = seq * (SUB * LANES) + part * LANES
            times = times + lax.broadcasted_iota(jnp.int32, (LANES, n_seq), 0)
            alive = times < limit_ref[0]
            z = jnp.where(alive, z_in[at, cut].astype(jnp.float32), 0.0)
            g = cot_in[at, cut].astype(jnp.float32) * gate_in[at, cut].astype(jnp.float32)
            g = jnp.where(alive, g, 0.0)
            g_keep[at, cut] = g.astype(jnp.bfloat16)
            top = column * n_seq * 2 * SUB + part
            stage[pl.ds(top, n_seq, stride=2 * SUB), :] = z.T
            stage[pl.ds(top + SUB, n_seq, stride=2 * SUB), :] = g.T
            return carry

        lax.fori_loop(0, SUB, turn_zg, 0)
        pack(column, zg_ref.at[:, column])

    @pl.when(core == user)
    def _():
        pl.semaphore_wait(barrier, n_seq - 1)

    @pl.when(core != user)
    def _():
        pl.semaphore_wait(barrier, n_seq)

    scatter(0, lambda target: zg_ref.at[target], zbuf.at[user, seq])

    inputs[3].wait()
    for column in range(PER):
        cut = slice(column * n_seq, (column + 1) * n_seq)
        for kind in range(2):
            wide[kind, :, :n_seq] = h_in[kind, :, cut].astype(jnp.float32)

        def turn_h(low_bits, carry, column=column):
            for kind in range(2):
                tile = wide[kind, pl.ds(low_bits, LANES, stride=SUB), :]
                first = column * n_seq * 2 * SUB + kind * SUB + low_bits
                stage[pl.ds(first, n_seq, stride=2 * SUB), :] = tile.T[:n_seq]
            return carry

        lax.fori_loop(0, SUB, turn_h, 0)
        pack(column, h_ref.at[:, column])
    scatter(3, lambda target: h_ref.at[target], hbuf.at[seq])

    for load in loads:
        load.wait()

    mate = {"seq": seq + 1 - 2 * core, "user": user}

    arrived = zbuf.at[core]
    await_all(arrived, recv_sems.at[0])
    swap = remote(arrived, arrived, 1, mate)
    swap.start()
    swap.wait()

    def cross(channel):
        return remote(s_cross.at[channel], s_send.at[:, core, channel], 4 + channel, mate)

    def forward(channel, carry):
        def fill(part, inner_carry):
            for who in range(2):
                tile = zbuf[who, pl.ds(part * groups, groups), channel]
                tile = tile.astype(jnp.float32)
                at = pl.ds(pl.multiple_of(part * block, block), block)
                for kind in range(2):
                    piece = tile[:, kind * SUB : (kind + 1) * SUB, :]
                    piece = piece.reshape(block, LANES).astype(jnp.bfloat16)
                    left = (2 * who + kind) * LANES
                    x_buf[at, left : left + LANES] = piece
            return inner_carry

        lax.fori_loop(0, blocks, fill, 0)

        def spectrum(part, inner_carry):
            start = pl.multiple_of(part * block, block)
            at = pl.ds(start, block)
            below = pl.ds(pl.multiple_of(rows + part * block, block), block)
            x = x_buf[...]
            dot = functools.partial(jnp.dot, preferred_element_type=jnp.float32)
            y_real = dot(m_high[at, :], x) + dot(m_low[at, :], x)
            y_imag = dot(m_high[below, :], x) + dot(m_low[below, :], x)
            t_real, t_imag = m_turn[0, at, :], m_turn[1, at, :]
            s_real = s_imag = None
            for who in range(2):
                spectra = []
                for kind in range(2):
                    left = (2 * who + kind) * LANES
                    a_real = y_real[:, left : left + LANES]
                    a_imag = y_imag[:, left : left + LANES]
                    mid = jnp.concatenate(
                        [a_real * t_real - a_imag * t_imag, a_real * t_imag + a_imag * t_real],
                        axis=1,
                    ).astype(jnp.bfloat16)
                    spectra.append(dot(mid, m_inner[0]) + dot(mid, m_inner[1]))
                z, g = spectra
                g_buf[channel, who, at, :] = g
                z_real, z_imag = z[:, :LANES], z[:, LANES:]
                g_real, g_imag = g[:, :LANES], g[:, LANES:]
                c_real = z_real * g_real + z_imag * g_imag
                c_imag = z_real * g_imag - z_imag * g_real
                s_real = c_real if who == 0 else s_real + c_real
                s_imag = c_imag if who == 0 else s_imag + c_imag
            s_real, s_imag = s_real * scale, s_imag * scale
            half = LANES // 2
            outs = []
            for who in range(2):
                cut = slice(who * half, (who + 1) * half)
                out = jnp.concatenate([s_real[:, cut], s_imag[:, cut]], axis=1)
                outs.append(out.reshape(groups, SUB, LANES))
            here = pl.ds(part * groups, groups)
            s_send[here, core, channel] = jnp.where(core == 0, outs[0], outs[1]).astype(jnp.bfloat16)
            s_cross[channel, here] = jnp.where(core == 0, outs[1], outs[0]).astype(jnp.bfloat16)
            return inner_carry

        lax.fori_loop(0, blocks, spectrum, 0)
        cross(channel).start()
        return carry

    lax.fori_loop(0, PER, forward, 0)

    for channel in range(PER):
        cross(channel).wait()

    def gather(which, src, dst):
        def put(there, bit):
            to = {"seq": 2 * there + bit, "user": core}
            remote(src.at[2 * there + bit], dst.at[chip], which, to).start()

        @pl.when(core == user)
        def _():
            pltpu.make_async_copy(src.at[seq], dst.at[chip], recv_sems.at[which]).start()

        @pl.when(core != user)
        def _():
            put(place, core)

        visit(n_seq, place, core, put)

    gather(7, s_send, s_out)

    await_all(hbuf, recv_sems.at[3])

    def inverse(channel, carry):
        dot = functools.partial(jnp.dot, preferred_element_type=jnp.float32)

        def product(part, inner_carry):
            at = pl.ds(pl.multiple_of(part * block, block), block)
            below = pl.ds(pl.multiple_of(rows + part * block, block), block)
            tile = hbuf[pl.ds(part * groups, groups), channel].astype(jnp.float32)
            h_real = tile[:, :SUB, :].reshape(block, LANES)
            h_imag = tile[:, SUB:, :].reshape(block, LANES)
            t_real, t_imag = m_turn[0, at, :], m_turn[1, at, :]
            for who in range(2):
                g = g_buf[channel, who, at, :]
                g_real, g_imag = g[:, :LANES], g[:, LANES:]
                q = jnp.concatenate(
                    [h_real * g_real + h_imag * g_imag, h_real * g_imag - h_imag * g_real],
                    axis=1,
                ).astype(jnp.bfloat16)
                b = dot(q, m_inner[2]) + dot(q, m_inner[3])
                b_real, b_imag = b[:, :LANES], b[:, LANES:]
                left = who * LANES
                b_buf[at, left : left + LANES] = (b_real * t_real + b_imag * t_imag).astype(
                    jnp.bfloat16
                )
                b_buf[below, left : left + LANES] = (b_imag * t_real - b_real * t_imag).astype(
                    jnp.bfloat16
                )
            return inner_carry

        lax.fori_loop(0, blocks, product, 0)

        def fold(part, inner_carry):
            at = pl.ds(pl.multiple_of(part * block, block), block)
            conv = dot(m_back[at, :], b_buf[...]) * scale
            for who in range(2):
                piece = conv[:, who * LANES : (who + 1) * LANES]
                c_part[who, pl.ds(part * groups, groups), channel] = piece.reshape(
                    groups, SUB, LANES
                )
            return inner_carry

        lax.fori_loop(0, blocks, fold, 0)
        return carry

    lax.fori_loop(0, PER, inverse, 0)

    swap_back = remote(c_part.at[1 - core], c_other, 8, mate)
    swap_back.start()
    swap_back.wait()

    def join(part, carry):
        at = pl.ds(part * groups, groups)
        c_send[at] = (c_part[core, at] + c_other[at]).astype(jnp.bfloat16)
        return carry

    lax.fori_loop(0, blocks, join, 0)

    gather(9, c_send, c_out)

    def unpack(column, src):
        size = n_seq * SUB // 4

        def body(part, carry):
            tile = src[pl.ds(part * (n_seq // 4), n_seq // 4)].astype(jnp.float32)
            first = pl.multiple_of(column * n_seq * SUB + part * size, 8)
            stage[pl.ds(first, size), :] = tile.reshape(size, LANES)
            return carry

        lax.fori_loop(0, 4, body, 0)

    half = LANES // 2
    await_all(s_out, recv_sems.at[7])
    for parity in range(2):
        for column in range(PER):
            cut = slice(column * n_seq, (column + 1) * n_seq)
            unpack(column, s_out.at[:, parity, column])

            def turn_s(low_bits, carry, column=column):
                first = column * n_seq * SUB + low_bits
                tile = stage[pl.ds(first, n_seq, stride=SUB), :].T
                for kind in range(2):
                    piece = tile[kind * half : (kind + 1) * half]
                    first = kind * half * SUB + low_bits
                    wide[column, pl.ds(first, half, stride=SUB), :n_seq] = piece
                return carry

            lax.fori_loop(0, SUB, turn_s, 0)
            for kind in range(2):
                at = pl.ds(kind * half * SUB, half * SUB)
                s_final[parity, kind, 0, :, cut] = wide[column, at, :n_seq]

    await_all(c_out, recv_sems.at[9])
    for column in range(PER):
        unpack(column, c_out.at[:, column])

    def finish(part, carry):
        at = pl.ds(pl.multiple_of(part * LANES, LANES), LANES)
        times = seq * (SUB * LANES) + part * LANES
        times = times + lax.broadcasted_iota(jnp.int32, (LANES, n_seq), 0)
        alive = times < limit_ref[0]
        for column in range(PER):
            cut = slice(column * n_seq, (column + 1) * n_seq)
            conv = stage[pl.ds(column * n_seq * SUB + part, n_seq, stride=SUB), :].T
            total = gain_ref[cut][None, :] * g_keep[at, cut].astype(jnp.float32) + conv
            z_final[0, at, cut] = jnp.where(alive, total, 0.0).astype(jnp.bfloat16)
        return carry

    lax.fori_loop(0, SUB, finish, 0)

    await_sent(0, lambda count: zg_ref.at[pl.ds(0, count)])
    await_sent(3, lambda count: h_ref.at[pl.ds(0, count)])
    await_sent(7, lambda count: s_send.at[pl.ds(0, count)])
    await_sent(9, lambda count: c_send.at[pl.ds(0, count)])


def mixer(n_seq, z_input, gate_input, cotangent, spectrum, skip_gain, lengths):
    rows = SUB * n_seq
    span, channels = z_input.shape[1:]
    bf16, f32 = jnp.bfloat16, jnp.float32
    high, low, back, turn, inner = (jnp.asarray(t) for t in tables(n_seq))
    anywhere = pl.BlockSpec(memory_space=pl.ANY)
    return pl.pallas_call(
        functools.partial(kernel, n_seq),
        out_shape=(
            pltpu.VMEM((2, 2, 1, span // 2, channels), f32),
            pltpu.VMEM((1, span, channels), bf16),
        ),
        in_specs=[anywhere] * 4
        + [pl.BlockSpec(memory_space=pltpu.SMEM), pl.BlockSpec(memory_space=pltpu.VMEM)]
        + [anywhere] * 5,
        out_specs=(pl.BlockSpec(memory_space=pltpu.VMEM),) * 2,
        scratch_shapes=[
            pltpu.VMEM((span, channels), bf16),
            pltpu.VMEM((span, channels), bf16),
            pltpu.VMEM((span, channels), bf16),
            pltpu.VMEM((2, span, channels), bf16),
            pltpu.VMEM((channels * 2 * SUB, LANES), f32),
            pltpu.VMEM((PER, span, LANES), f32),
            pltpu.VMEM((n_seq, PER, 2 * SUB, LANES), bf16),
            pltpu.VMEM((n_seq, PER, 2 * SUB, LANES), bf16),
            pltpu.VMEM((n_seq, 2, PER, SUB, LANES), bf16),
            pltpu.VMEM((n_seq, PER, SUB, LANES), bf16),
            pltpu.VMEM((span, channels), bf16),
            pltpu.VMEM((2, n_seq, PER, 2 * SUB, LANES), bf16),
            pltpu.VMEM((n_seq, PER, 2 * SUB, LANES), bf16),
            pltpu.VMEM((2 * rows, rows), bf16),
            pltpu.VMEM((2 * rows, rows), bf16),
            pltpu.VMEM((rows, 2 * rows), bf16),
            pltpu.VMEM((2, rows, LANES), f32),
            pltpu.VMEM((4, 2 * LANES, 2 * LANES), bf16),
            pltpu.VMEM((rows, 4 * LANES), bf16),
            pltpu.VMEM((PER, 2, rows, 2 * LANES), f32),
            pltpu.VMEM((2 * rows, 2 * LANES), bf16),
            pltpu.VMEM((n_seq, 2, PER, SUB, LANES), bf16),
            pltpu.VMEM((PER, n_seq, SUB, LANES), bf16),
            pltpu.VMEM((2, n_seq, PER, SUB, LANES), f32),
            pltpu.VMEM((n_seq, PER, SUB, LANES), f32),
            pltpu.VMEM((n_seq, PER, SUB, LANES), bf16),
            pltpu.SemaphoreType.DMA((4,)),
            pltpu.SemaphoreType.DMA((5,)),
            pltpu.SemaphoreType.DMA((10,)),
            pltpu.SemaphoreType.DMA((10,)),
        ],
        compiler_params=pltpu.CompilerParams(
            collective_id=0, has_side_effects=True, vmem_limit_bytes=52 * 1024 * 1024
        ),
    )(z_input, gate_input, cotangent, spectrum, lengths, skip_gain, high, low, back, turn, inner)


def store(s_ref, z_ref, s_out, z_out, sems):
    copies = [pltpu.make_async_copy(z_ref, z_out, sems.at[4])]
    for parity in range(2):
        for kind in range(2):
            src, dst = s_ref.at[parity, kind], s_out.at[parity, kind]
            copies.append(pltpu.make_async_copy(src, dst, sems.at[2 * parity + kind]))
    for copy in copies:
        copy.start()
    for copy in copies:
        copy.wait()


def settle(s_rows, z_grad):
    held = [pltpu.with_memory_space_constraint(a, pltpu.VMEM) for a in (s_rows, z_grad)]
    return pl.pallas_call(
        store,
        out_shape=tuple(jax.ShapeDtypeStruct(a.shape, a.dtype) for a in (s_rows, z_grad)),
        in_specs=[pl.BlockSpec(memory_space=pl.ANY)] * 2,
        out_specs=(pl.BlockSpec(memory_space=pltpu.HBM),) * 2,
        scratch_shapes=[pltpu.SemaphoreType.DMA((5,))],
        compiler_params=pltpu.CompilerParams(vmem_limit_bytes=4 * 1024 * 1024),
    )(*held)


def on_device(z_input, gate_input, cotangent, spectrum, skip_gain, lengths):
    n_seq = lax.axis_size("seq")
    s_rows, z_grad = mixer(
        n_seq, z_input, gate_input, cotangent, spectrum, skip_gain, lengths
    )
    spectrum_grad, z_grad = settle(s_rows, z_grad)
    return (z_grad, spectrum_grad)


def solution(mesh):
    return jax.shard_map(
        on_device,
        mesh=mesh,
        in_specs=(
            P("user", "seq", None),
            P("user", "seq", None),
            P("user", "seq", None),
            P(None, None, "seq", None, None),
            P(),
            P("user"),
        ),
        out_specs=(P("user", "seq", None), P(None, None, "seq", "user", None)),
        check_vma=False,
    )
```

```python
import functools

import jax
import jax.numpy as jnp
import ml_dtypes
import numpy as np
from jax import lax
from jax.experimental import pallas as pl
from jax.experimental.pallas import tpu as pltpu
from jax.sharding import PartitionSpec as P

LANES = 128
SUB = 8
PER = 3


def split_bf16(values):
    high = values.astype(ml_dtypes.bfloat16)
    low = (values - high.astype(np.float64)).astype(ml_dtypes.bfloat16)
    return high, low


def tables(n_seq):
    rows = SUB * n_seq
    total = rows * LANES
    index = np.arange(rows)
    freq = (index // SUB) + n_seq * (index % SUB)
    outer, turn = [], []
    for parity in range(2):
        twice = 2 * freq + parity
        angle = (twice[:, None] * index[None, :]) % (2 * rows) * (np.pi / rows)
        outer.append(np.concatenate([np.cos(angle), -np.sin(angle)], 0))
        small = twice[:, None] * np.arange(LANES)[None, :] * (np.pi / total)
        turn.append(np.stack([np.cos(small), -np.sin(small)]))
    outer = np.stack(outer)
    high, low = split_bf16(outer)
    back = np.ascontiguousarray(high.transpose(0, 2, 1))
    lane = np.arange(LANES)
    angle = (lane[:, None] * lane[None, :]) % LANES * (2 * np.pi / LANES)
    cos, sin = np.cos(angle), np.sin(angle)
    forward = np.block([[cos, -sin], [sin, cos]])
    inverse = np.block([[cos, sin], [-sin, cos]])
    fwd_high, fwd_low = split_bf16(forward)
    inv_high, inv_low = split_bf16(inverse)
    inner = np.stack([fwd_high, fwd_low, inv_high, inv_low])
    return high, low, back, np.stack(turn).astype(np.float32), inner


def visit(n_seq, place, bit, act):
    places = n_seq // 2
    planes = 8 if places % 8 == 0 else 1
    inner = places // planes

    def group(step, skip):
        for plane in range(planes):
            there = place + step + (plane * 3 % planes) * inner
            there = jnp.where(there >= places, there - places, there)
            if plane or not skip:
                act(there, bit)
            act(there, 1 - bit)

    group(0, True)

    def body(step, carry):
        group(step, False)
        return carry

    lax.fori_loop(1, inner, body, 0)


def kernel(
    n_seq,
    z_hbm,
    gate_hbm,
    cot_hbm,
    h_hbm,
    limit_ref,
    gain_ref,
    high_ref,
    low_ref,
    back_ref,
    turn_ref,
    inner_ref,
    s_final,
    z_final,
    z_in,
    gate_in,
    cot_in,
    h_in,
    stage,
    wide,
    zg_ref,
    h_ref,
    s_out,
    c_out,
    g_keep,
    zbuf,
    hbuf,
    m_high,
    m_low,
    m_back,
    m_turn,
    m_inner,
    x_buf,
    g_buf,
    b_buf,
    s_send,
    s_cross,
    c_part,
    c_other,
    c_send,
    input_sems,
    table_sems,
    send_sems,
    recv_sems,
):
    rows = SUB * n_seq
    block = min(256, rows)
    groups = block // SUB
    blocks = rows // block
    scale = 1.0 / (2.0 * rows * LANES)
    seq = lax.axis_index("seq")
    user = lax.axis_index("user")
    core = lax.rem(seq, 2)
    place = seq // 2
    chip = place * 2 + user

    def remote(src, dst, which, device):
        return pltpu.make_async_remote_copy(
            src_ref=src,
            dst_ref=dst,
            send_sem=send_sems.at[which],
            recv_sem=recv_sems.at[which],
            device_id=device,
            device_id_type=pl.DeviceIdType.MESH,
        )

    def await_all(ref, sem):
        pltpu.make_async_copy(ref, ref, sem).wait()

    def await_sent(which, some):
        @pl.when(core == user)
        def _():
            await_all(some(n_seq - 1), send_sems.at[which])

        @pl.when(core != user)
        def _():
            await_all(some(n_seq), send_sems.at[which])

    inputs = [
        pltpu.make_async_copy(z_hbm.at[0], z_in, input_sems.at[0]),
        pltpu.make_async_copy(gate_hbm.at[0], gate_in, input_sems.at[1]),
        pltpu.make_async_copy(cot_hbm.at[0], cot_in, input_sems.at[2]),
        pltpu.make_async_copy(h_hbm.at[user, :, 0], h_in, input_sems.at[3]),
    ]
    loads = [
        pltpu.make_async_copy(high_ref.at[core], m_high, table_sems.at[0]),
        pltpu.make_async_copy(low_ref.at[core], m_low, table_sems.at[1]),
        pltpu.make_async_copy(back_ref.at[core], m_back, table_sems.at[2]),
        pltpu.make_async_copy(turn_ref.at[core], m_turn, table_sems.at[3]),
        pltpu.make_async_copy(inner_ref, m_inner, table_sems.at[4]),
    ]
    for load in inputs[:3]:
        load.start()

    barrier = pltpu.get_barrier_semaphore()

    def greet(there, bit):
        pl.semaphore_signal(
            barrier,
            inc=1,
            device_id={"seq": 2 * there + bit, "user": core},
            device_id_type=pl.DeviceIdType.MESH,
        )

    @pl.when(core != user)
    def _():
        greet(place, core)

    visit(n_seq, place, core, greet)
    for load in inputs[3:] + loads:
        load.start()

    channels = PER * n_seq
    for load in inputs[:3]:
        load.wait()

    def pack(column, dst):
        size = n_seq * 2 * SUB // 4

        def body(part, carry):
            first = pl.multiple_of(column * n_seq * 2 * SUB + part * size, 8)
            tile = stage[pl.ds(first, size), :].reshape(n_seq // 4, 2 * SUB, LANES)
            dst[pl.ds(part * (n_seq // 4), n_seq // 4)] = tile.astype(jnp.bfloat16)
            return carry

        lax.fori_loop(0, 4, body, 0)

    def scatter(which, src, dst):
        def put(there, bit):
            to = {"seq": 2 * there + user, "user": bit}
            remote(src(2 * there + bit), dst, which, to).start()

        @pl.when(core == user)
        def _():
            pltpu.make_async_copy(src(chip), dst, recv_sems.at[which]).start()

        @pl.when(core != user)
        def _():
            put(place, user)

        visit(n_seq, place, user, put)

    for column in range(PER):
        cut = slice(column * n_seq, (column + 1) * n_seq)

        def turn_zg(part, carry, column=column, cut=cut):
            at = pl.ds(pl.multiple_of(part * LANES, LANES), LANES)
            times = seq * (SUB * LANES) + part * LANES
            times = times + lax.broadcasted_iota(jnp.int32, (LANES, n_seq), 0)
            alive = times < limit_ref[0]
            z = jnp.where(alive, z_in[at, cut].astype(jnp.float32), 0.0)
            g = cot_in[at, cut].astype(jnp.float32) * gate_in[at, cut].astype(jnp.float32)
            g = jnp.where(alive, g, 0.0)
            g_keep[at, cut] = g.astype(jnp.bfloat16)
            top = column * n_seq * 2 * SUB + part
            stage[pl.ds(top, n_seq, stride=2 * SUB), :] = z.T
            stage[pl.ds(top + SUB, n_seq, stride=2 * SUB), :] = g.T
            return carry

        lax.fori_loop(0, SUB, turn_zg, 0)
        pack(column, zg_ref.at[:, column])

    @pl.when(core == user)
    def _():
        pl.semaphore_wait(barrier, n_seq - 1)

    @pl.when(core != user)
    def _():
        pl.semaphore_wait(barrier, n_seq)

    scatter(0, lambda target: zg_ref.at[target], zbuf.at[user, seq])

    inputs[3].wait()
    for column in range(PER):
        cut = slice(column * n_seq, (column + 1) * n_seq)
        for kind in range(2):
            wide[kind, : SUB * LANES, :n_seq] = h_in[kind, :, cut].astype(jnp.float32)

        def turn_h(low_bits, carry, column=column):
            for kind in range(2):
                tile = wide[kind, pl.ds(low_bits, LANES, stride=SUB), :]
                first = column * n_seq * 2 * SUB + kind * SUB + low_bits
                stage[pl.ds(first, n_seq, stride=2 * SUB), :] = tile.T[:n_seq]
            return carry

        lax.fori_loop(0, SUB, turn_h, 0)
        pack(column, h_ref.at[:, column])
    scatter(3, lambda target: h_ref.at[target], hbuf.at[seq])

    for load in loads:
        load.wait()

    mate = {"seq": seq + 1 - 2 * core, "user": user}

    arrived = zbuf.at[core]
    await_all(arrived, recv_sems.at[0])
    swap = remote(arrived, arrived, 1, mate)
    swap.start()
    swap.wait()

    def cross(channel):
        return remote(s_cross.at[channel], s_send.at[:, core, channel], 4 + channel, mate)

    def forward(channel, carry):
        def fill(part, inner_carry):
            for who in range(2):
                tile = zbuf[who, pl.ds(part * groups, groups), channel]
                tile = tile.astype(jnp.float32)
                at = pl.ds(pl.multiple_of(part * block, block), block)
                for kind in range(2):
                    piece = tile[:, kind * SUB : (kind + 1) * SUB, :]
                    piece = piece.reshape(block, LANES).astype(jnp.bfloat16)
                    left = (2 * who + kind) * LANES
                    x_buf[at, left : left + LANES] = piece
            return inner_carry

        lax.fori_loop(0, blocks, fill, 0)

        def spectrum(part, inner_carry):
            start = pl.multiple_of(part * block, block)
            at = pl.ds(start, block)
            below = pl.ds(pl.multiple_of(rows + part * block, block), block)
            x = x_buf[...]
            dot = functools.partial(jnp.dot, preferred_element_type=jnp.float32)
            y_real = dot(m_high[at, :], x) + dot(m_low[at, :], x)
            y_imag = dot(m_high[below, :], x) + dot(m_low[below, :], x)
            t_real, t_imag = m_turn[0, at, :], m_turn[1, at, :]
            s_real = s_imag = None
            for who in range(2):
                spectra = []
                for kind in range(2):
                    left = (2 * who + kind) * LANES
                    a_real = y_real[:, left : left + LANES]
                    a_imag = y_imag[:, left : left + LANES]
                    mid = jnp.concatenate(
                        [a_real * t_real - a_imag * t_imag, a_real * t_imag + a_imag * t_real],
                        axis=1,
                    ).astype(jnp.bfloat16)
                    spectra.append(dot(mid, m_inner[0]) + dot(mid, m_inner[1]))
                z, g = spectra
                g_buf[channel, who, at, :] = g
                z_real, z_imag = z[:, :LANES], z[:, LANES:]
                g_real, g_imag = g[:, :LANES], g[:, LANES:]
                c_real = z_real * g_real + z_imag * g_imag
                c_imag = z_real * g_imag - z_imag * g_real
                s_real = c_real if who == 0 else s_real + c_real
                s_imag = c_imag if who == 0 else s_imag + c_imag
            s_real, s_imag = s_real * scale, s_imag * scale
            half = LANES // 2
            outs = []
            for who in range(2):
                cut = slice(who * half, (who + 1) * half)
                out = jnp.concatenate([s_real[:, cut], s_imag[:, cut]], axis=1)
                outs.append(out.reshape(groups, SUB, LANES))
            here = pl.ds(part * groups, groups)
            s_send[here, core, channel] = jnp.where(core == 0, outs[0], outs[1]).astype(jnp.bfloat16)
            s_cross[channel, here] = jnp.where(core == 0, outs[1], outs[0]).astype(jnp.bfloat16)
            return inner_carry

        lax.fori_loop(0, blocks, spectrum, 0)
        cross(channel).start()
        return carry

    lax.fori_loop(0, PER, forward, 0)

    for channel in range(PER):
        cross(channel).wait()

    def gather(which, src, dst):
        def put(there, bit):
            to = {"seq": 2 * there + bit, "user": core}
            remote(src.at[2 * there + bit], dst.at[chip], which, to).start()

        @pl.when(core == user)
        def _():
            pltpu.make_async_copy(src.at[seq], dst.at[chip], recv_sems.at[which]).start()

        @pl.when(core != user)
        def _():
            put(place, core)

        visit(n_seq, place, core, put)

    gather(7, s_send, s_out)

    await_all(hbuf, recv_sems.at[3])

    def inverse(channel, carry):
        dot = functools.partial(jnp.dot, preferred_element_type=jnp.float32)

        def product(part, inner_carry):
            at = pl.ds(pl.multiple_of(part * block, block), block)
            below = pl.ds(pl.multiple_of(rows + part * block, block), block)
            tile = hbuf[pl.ds(part * groups, groups), channel].astype(jnp.float32)
            h_real = tile[:, :SUB, :].reshape(block, LANES)
            h_imag = tile[:, SUB:, :].reshape(block, LANES)
            t_real, t_imag = m_turn[0, at, :], m_turn[1, at, :]
            for who in range(2):
                g = g_buf[channel, who, at, :]
                g_real, g_imag = g[:, :LANES], g[:, LANES:]
                q = jnp.concatenate(
                    [h_real * g_real + h_imag * g_imag, h_real * g_imag - h_imag * g_real],
                    axis=1,
                ).astype(jnp.bfloat16)
                b = dot(q, m_inner[2]) + dot(q, m_inner[3])
                b_real, b_imag = b[:, :LANES], b[:, LANES:]
                left = who * LANES
                b_buf[at, left : left + LANES] = (b_real * t_real + b_imag * t_imag).astype(
                    jnp.bfloat16
                )
                b_buf[below, left : left + LANES] = (b_imag * t_real - b_real * t_imag).astype(
                    jnp.bfloat16
                )
            return inner_carry

        lax.fori_loop(0, blocks, product, 0)

        def fold(part, inner_carry):
            at = pl.ds(pl.multiple_of(part * block, block), block)
            conv = dot(m_back[at, :], b_buf[...]) * scale
            for who in range(2):
                piece = conv[:, who * LANES : (who + 1) * LANES]
                c_part[who, pl.ds(part * groups, groups), channel] = piece.reshape(
                    groups, SUB, LANES
                )
            return inner_carry

        lax.fori_loop(0, blocks, fold, 0)
        return carry

    lax.fori_loop(0, PER, inverse, 0)

    swap_back = remote(c_part.at[1 - core], c_other, 8, mate)
    swap_back.start()
    swap_back.wait()

    def join(part, carry):
        at = pl.ds(part * groups, groups)
        c_send[at] = (c_part[core, at] + c_other[at]).astype(jnp.bfloat16)
        return carry

    lax.fori_loop(0, blocks, join, 0)

    gather(9, c_send, c_out)

    def unpack(column, src):
        size = n_seq * SUB // 4

        def body(part, carry):
            tile = src[pl.ds(part * (n_seq // 4), n_seq // 4)].astype(jnp.float32)
            first = pl.multiple_of(column * n_seq * SUB + part * size, 8)
            stage[pl.ds(first, size), :] = tile.reshape(size, LANES)
            return carry

        lax.fori_loop(0, 4, body, 0)

    half = LANES // 2
    await_all(s_out, recv_sems.at[7])
    for parity in range(2):
        for column in range(PER):
            cut = slice(column * n_seq, (column + 1) * n_seq)
            unpack(column, s_out.at[:, parity, column])

            def turn_s(low_bits, carry, column=column):
                first = column * n_seq * SUB + low_bits
                tile = stage[pl.ds(first, n_seq, stride=SUB), :].T
                for kind in range(2):
                    piece = tile[kind * half : (kind + 1) * half]
                    first = kind * half * SUB + low_bits
                    wide[column, pl.ds(first, half, stride=SUB), :n_seq] = piece
                return carry

            lax.fori_loop(0, SUB, turn_s, 0)
            for kind in range(2):
                at = pl.ds(kind * half * SUB, half * SUB)
                s_final[parity, kind, 0, :, cut] = wide[column, at, :n_seq]

    await_all(c_out, recv_sems.at[9])
    for column in range(PER):
        unpack(column, c_out.at[:, column])

    def finish(part, carry):
        at = pl.ds(pl.multiple_of(part * LANES, LANES), LANES)
        times = seq * (SUB * LANES) + part * LANES
        times = times + lax.broadcasted_iota(jnp.int32, (LANES, n_seq), 0)
        alive = times < limit_ref[0]
        for column in range(PER):
            cut = slice(column * n_seq, (column + 1) * n_seq)
            conv = stage[pl.ds(column * n_seq * SUB + part, n_seq, stride=SUB), :].T
            total = gain_ref[cut][None, :] * g_keep[at, cut].astype(jnp.float32) + conv
            z_final[0, at, cut] = jnp.where(alive, total, 0.0).astype(jnp.bfloat16)
        return carry

    lax.fori_loop(0, SUB, finish, 0)

    await_sent(0, lambda count: zg_ref.at[pl.ds(0, count)])
    await_sent(3, lambda count: h_ref.at[pl.ds(0, count)])
    await_sent(7, lambda count: s_send.at[pl.ds(0, count)])
    await_sent(9, lambda count: c_send.at[pl.ds(0, count)])


def mixer(n_seq, z_input, gate_input, cotangent, spectrum, skip_gain, lengths):
    rows = SUB * n_seq
    span, channels = z_input.shape[1:]
    bf16, f32 = jnp.bfloat16, jnp.float32
    high, low, back, turn, inner = (jnp.asarray(t) for t in tables(n_seq))
    anywhere = pl.BlockSpec(memory_space=pl.ANY)
    return pl.pallas_call(
        functools.partial(kernel, n_seq),
        out_shape=(
            pltpu.VMEM((2, 2, 1, span // 2, channels), f32),
            pltpu.VMEM((1, span, channels), bf16),
        ),
        in_specs=[anywhere] * 4
        + [pl.BlockSpec(memory_space=pltpu.SMEM), pl.BlockSpec(memory_space=pltpu.VMEM)]
        + [anywhere] * 5,
        out_specs=(pl.BlockSpec(memory_space=pltpu.VMEM),) * 2,
        scratch_shapes=[
            pltpu.VMEM((span, channels), bf16),
            pltpu.VMEM((span, channels), bf16),
            pltpu.VMEM((span, channels), bf16),
            pltpu.VMEM((2, span, channels), bf16),
            pltpu.VMEM(((channels + 1) * 2 * SUB, LANES), f32),
            pltpu.VMEM((PER, span + SUB, LANES), f32),
            pltpu.VMEM((n_seq, PER, 2 * SUB, LANES), bf16),
            pltpu.VMEM((n_seq, PER, 2 * SUB, LANES), bf16),
            pltpu.VMEM((n_seq, 2, PER, SUB, LANES), bf16),
            pltpu.VMEM((n_seq, PER, SUB, LANES), bf16),
            pltpu.VMEM((span, channels), bf16),
            pltpu.VMEM((2, n_seq, PER, 2 * SUB, LANES), bf16),
            pltpu.VMEM((n_seq, PER, 2 * SUB, LANES), bf16),
            pltpu.VMEM((2 * rows, rows), bf16),
            pltpu.VMEM((2 * rows, rows), bf16),
            pltpu.VMEM((rows, 2 * rows), bf16),
            pltpu.VMEM((2, rows, LANES), f32),
            pltpu.VMEM((4, 2 * LANES, 2 * LANES), bf16),
            pltpu.VMEM((rows, 4 * LANES), bf16),
            pltpu.VMEM((PER, 2, rows, 2 * LANES), f32),
            pltpu.VMEM((2 * rows, 2 * LANES), bf16),
            pltpu.VMEM((n_seq, 2, PER, SUB, LANES), bf16),
            pltpu.VMEM((PER, n_seq, SUB, LANES), bf16),
            pltpu.VMEM((2, n_seq, PER, SUB, LANES), f32),
            pltpu.VMEM((n_seq, PER, SUB, LANES), f32),
            pltpu.VMEM((n_seq, PER, SUB, LANES), bf16),
            pltpu.SemaphoreType.DMA((4,)),
            pltpu.SemaphoreType.DMA((5,)),
            pltpu.SemaphoreType.DMA((10,)),
            pltpu.SemaphoreType.DMA((10,)),
        ],
        compiler_params=pltpu.CompilerParams(
            collective_id=0, has_side_effects=True, vmem_limit_bytes=52 * 1024 * 1024
        ),
    )(z_input, gate_input, cotangent, spectrum, lengths, skip_gain, high, low, back, turn, inner)


def store(s_ref, z_ref, s_out, z_out, sems):
    copies = [pltpu.make_async_copy(z_ref, z_out, sems.at[4])]
    for parity in range(2):
        for kind in range(2):
            src, dst = s_ref.at[parity, kind], s_out.at[parity, kind]
            copies.append(pltpu.make_async_copy(src, dst, sems.at[2 * parity + kind]))
    for copy in copies:
        copy.start()
    for copy in copies:
        copy.wait()


def settle(s_rows, z_grad):
    held = [pltpu.with_memory_space_constraint(a, pltpu.VMEM) for a in (s_rows, z_grad)]
    return pl.pallas_call(
        store,
        out_shape=tuple(jax.ShapeDtypeStruct(a.shape, a.dtype) for a in (s_rows, z_grad)),
        in_specs=[pl.BlockSpec(memory_space=pl.ANY)] * 2,
        out_specs=(pl.BlockSpec(memory_space=pltpu.HBM),) * 2,
        scratch_shapes=[pltpu.SemaphoreType.DMA((5,))],
        compiler_params=pltpu.CompilerParams(vmem_limit_bytes=4 * 1024 * 1024),
    )(*held)


def on_device(z_input, gate_input, cotangent, spectrum, skip_gain, lengths):
    n_seq = lax.axis_size("seq")
    s_rows, z_grad = mixer(
        n_seq, z_input, gate_input, cotangent, spectrum, skip_gain, lengths
    )
    spectrum_grad, z_grad = settle(s_rows, z_grad)
    return (z_grad, spectrum_grad)


def solution(mesh):
    return jax.shard_map(
        on_device,
        mesh=mesh,
        in_specs=(
            P("user", "seq", None),
            P("user", "seq", None),
            P("user", "seq", None),
            P(None, None, "seq", None, None),
            P(),
            P("user"),
        ),
        out_specs=(P("user", "seq", None), P(None, None, "seq", "user", None)),
        check_vma=False,
    )
```
